128 devices in a mesh: dev: 128 (over z, y, x, core).
Axes of the slice: x: 4, y: 4, z: 4, core: 2. Of those that a mesh axis runs over, the one named last changes fastest.
Arguments:
- emb: bfloat16 [131072, 768], P('dev')
- cluster: int32 [131072], P('dev'), may hold values from 0 to 1023, as said below
- rank: int32 [131072], P('dev'), may hold values from 0 to 262143, as said below
Outputs:
- nearest: float32 [131072], P('dev')
The draws below stay inside these ranges and needn't reach their ends.
Inputs may be any that keep to these rules, and one draw needn't show every extreme that they name: Item i is placed on device (cluster[i] mod N + rank[i] mod 2) mod N of dev, N its number of devices (each cluster's items are split by rank parity over two neighbouring devices to bound the items any one device receives); the 1024 items of one device place at most 16 items on any one device, and exactly 16 on some device. `rank`: ranks are distinct over all items.
All inputs are finite; a program needn't handle non-finite values.
Results may differ from the reference program's by a relative error of at most 0.0005.
Values may be sent and summed in bfloat16 or wider, within the bound.
No kernel may reach another device: no remote copies, remote signals or barrier semaphores. Data moves between devices by JAX's collectives and lax.ppermute only.
A program may use at most 64 MiB of HBM per device.

```python
import math
import jax
import jax.numpy as jnp
from jax import lax

D = 768
ROWS_DEV = 1024
CLU_DEV = 8
ITEMS = 131072
CLUSTERS = 1024
CAP = 16
POOL = 2048
N_DEV = 128


def layout(key):
    base = jax.random.fold_in(key, 101)
    source_keys = jax.random.split(base, N_DEV)
    slot_owner = jnp.repeat(jnp.arange(N_DEV, dtype=jnp.int32), CAP)

    def per_source(source_key):
        key_order, key_first, key_shuffle = jax.random.split(source_key, 3)
        priority = jax.random.permutation(key_order, N_DEV * CAP).astype(jnp.int32)
        favored = jax.random.randint(key_first, (), 0, N_DEV)
        priority = priority + jnp.where(slot_owner == favored, 0, N_DEV * CAP).astype(jnp.int32)
        chosen = slot_owner[jnp.argsort(priority)[:ROWS_DEV]]
        return chosen[jax.random.permutation(key_shuffle, ROWS_DEV)]
    targets = jax.vmap(per_source)(source_keys).reshape(ITEMS)
    side_key, cluster_key = jax.random.split(jax.random.fold_in(base, 1))
    side = jax.random.randint(side_key, (ITEMS,), 0, 2).astype(jnp.int32)
    home = (targets - side) % N_DEV
    members = jax.random.randint(cluster_key, (ITEMS,), 0, CLU_DEV).astype(jnp.int32)
    return (side, (home + N_DEV * members).astype(jnp.int32))


def draw_cluster(key, part):
    side, cluster = layout(key)
    return cluster


def draw_rank(key, part):
    side, cluster = layout(key)
    key = jax.random.fold_in(key, 3)
    order_rank = jax.random.permutation(key, ITEMS).astype(jnp.int32)
    return (2 * order_rank + side).astype(jnp.int32)


def draw_emb(key, part):
    side, cluster = layout(key)
    key = jax.random.fold_in(key, 5)
    key_center, key_noise, key_mix, key_scale = jax.random.split(key, 4)
    centers = jax.random.normal(key_center, (CLUSTERS, D), jnp.float32)
    noise = jax.random.normal(key_noise, (ITEMS, D), jnp.float32)
    mixing = jax.random.uniform(key_mix, (ITEMS, 1), jnp.float32, 0.15, 0.85)
    scaling = jnp.exp(jax.random.uniform(key_scale, (ITEMS, 1), jnp.float32, 0.0, math.log(10.0)))
    return ((mixing * centers[cluster] + (1.0 - mixing) * noise) * scaling).astype(jnp.bfloat16)


def setup_inputs(seed: int = 0) -> dict:
    key_of = jax.random.split(jax.random.key(seed), 4)
    emb = draw_emb(jax.random.fold_in(key_of[3], 71), 0)
    cluster = draw_cluster(jax.random.fold_in(key_of[3], 71), 0)
    rank = draw_rank(jax.random.fold_in(key_of[3], 71), 0)
    return {"emb": emb, "cluster": cluster, "rank": rank}


def pool_view(sorted_unit, sorted_cluster, sorted_rank, offsets, arrivals, device):
    first = offsets[device]
    unit_part = lax.dynamic_slice_in_dim(sorted_unit, first, POOL, 0)
    cluster_part = lax.dynamic_slice_in_dim(sorted_cluster, first, POOL, 0)
    rank_part = lax.dynamic_slice_in_dim(sorted_rank, first, POOL, 0)
    live = jnp.arange(POOL, dtype=jnp.int32) < arrivals[device]
    cluster_part = jnp.where(live, cluster_part, -1)
    return (unit_part, cluster_part, rank_part)

def paired_best(left_unit, left_cluster, left_rank, right_unit, right_cluster, right_rank):
    similar = jnp.dot(left_unit.astype(jnp.float32), right_unit.astype(jnp.float32).T, precision=lax.Precision.HIGHEST)
    same_cluster = (left_cluster[:, None] == right_cluster[None, :]) & (right_cluster[None, :] >= 0)
    row_best = lax.optimization_barrier(jnp.max(jnp.where(same_cluster & (right_rank[None, :] < left_rank[:, None]), similar, -1.0), axis=1))
    column_best = lax.optimization_barrier(jnp.max(jnp.where(same_cluster & (left_rank[:, None] < right_rank[None, :]), similar, -1.0), axis=0))
    return (row_best, column_best)

def reference(emb, cluster, rank):
    widened = emb.astype(jnp.float32)
    unit_rows = (widened * lax.rsqrt(lax.optimization_barrier(jnp.sum(widened * widened, axis=-1, keepdims=True)) + 1e-06)).astype(jnp.bfloat16)
    target_dev = ((cluster % N_DEV + rank % 2) % N_DEV).astype(jnp.int32)
    sorted_index = jnp.argsort(target_dev, stable=True).astype(jnp.int32)
    arrivals = jnp.zeros((N_DEV,), jnp.int32).at[target_dev].add(1)
    offsets = (jnp.cumsum(arrivals) - arrivals).astype(jnp.int32)
    sorted_unit = jnp.concatenate([unit_rows[sorted_index], jnp.zeros((POOL, D), unit_rows.dtype)], axis=0)
    sorted_cluster = jnp.concatenate([cluster[sorted_index], jnp.full((POOL,), -1, jnp.int32)], axis=0)
    sorted_rank = jnp.concatenate([rank[sorted_index], jnp.zeros((POOL,), jnp.int32)], axis=0)

    def per_device(device):
        own = pool_view(sorted_unit, sorted_cluster, sorted_rank, offsets, arrivals, device)
        lower = pool_view(sorted_unit, sorted_cluster, sorted_rank, offsets, arrivals, (device - 1) % N_DEV)
        inner_best, unused = paired_best(*own, *own)
        cross_best, lower_extra = paired_best(*own, *lower)
        return (jnp.maximum(inner_best, cross_best), lower_extra)
    own_best, lower_extra = lax.map(per_device, jnp.arange(N_DEV, dtype=jnp.int32))
    combined = jnp.maximum(own_best, jnp.roll(lower_extra, -1, axis=0)).reshape(-1)
    position = jnp.zeros((ITEMS,), jnp.int32).at[sorted_index].set(jnp.arange(ITEMS, dtype=jnp.int32))
    flat_index = (target_dev * POOL + position - offsets[target_dev]).astype(jnp.int32)
    return combined[flat_index]
```

```python
import functools

import jax
import jax.numpy as jnp
from jax import lax
from jax.experimental import pallas as pl
from jax.experimental.pallas import tpu as pltpu
from jax.sharding import PartitionSpec as P

F32 = jnp.float32
BF16 = jnp.bfloat16
I32 = jnp.int32

N = 128
ROWS = 1024
D = 768
SLOTS = 10
MAIN = 8 * N
EXTRA = 2 * N
ALL = MAIN + EXTRA
NEAR = 176
FAR = 16
MOVED = 256
META = 128
HIGHEST = lax.Precision.HIGHEST
LIMIT = pltpu.CompilerParams(vmem_limit_bytes=56 * 1024 * 1024)


def iota(shape, dim):
    return lax.broadcasted_iota(I32, shape, dim)


def flag(mask, dtype=BF16):
    return jnp.where(mask, 1.0, 0.0).astype(dtype)


def dot(a, b, precision=None):
    return jnp.dot(a, b, preferred_element_type=F32, precision=precision)


def dot_nt(a, b, precision=None):
    return lax.dot_general(
        a, b, (((1,), (1,)), ((), ())), preferred_element_type=F32, precision=precision
    )


def pack_kernel(emb_ref, cluster_ref, rank_ref, out_ref, place_ref, unit, left, right):
    cluster = cluster_ref[...]
    rank = rank_ref[...]
    home = cluster % N
    member = cluster // N

    which = iota((N, ROWS), 0)
    at_home = which == home
    at_home_b = flag(at_home)
    chunks = jnp.concatenate([at_home_b[:, c * 128 : (c + 1) * 128] for c in range(8)], axis=0)
    lower = flag(iota((128, 128), 0) <= iota((128, 128), 1))
    running = dot(chunks, jnp.concatenate([lower, jnp.ones((128, 128), BF16)], axis=1))
    before = jnp.zeros((128, 128), F32)
    turn = []
    for c in range(8):
        part = running[c * 128 : (c + 1) * 128]
        turn.append(
            jnp.sum(
                jnp.where(at_home[:, c * 128 : (c + 1) * 128], part[:, :128] + before, 0.0),
                axis=0,
                keepdims=True,
            )
        )
        before = before + part[:, 128:]
    turn = jnp.concatenate(turn, axis=1) - 1.0

    count = dot_nt(jnp.ones((8, ROWS), BF16), at_home_b)
    window = count - float(SLOTS)
    queue = jnp.maximum(window, 0.0)
    for step in (1, 2, 4, 8, 16, 32, 64):
        queue = jnp.maximum(queue, window + pltpu.roll(queue, step, 1))
        window = window + pltpu.roll(window, step, 1)
    ahead = dot(pltpu.roll(queue, 1, 1), flag(at_home, F32), HIGHEST)[:1]
    offset = ahead + turn
    hops = jnp.floor((offset + 0.5) * (1.0 / SLOTS))
    slot = (offset - hops * SLOTS).astype(I32)
    hops = hops.astype(I32)
    target = (home + hops) % N
    place_ref[0:1, :] = home
    place_ref[1:2, :] = jnp.minimum(hops, 7) * 16 + slot

    for c in range(8):
        wide = emb_ref[c * 128 : (c + 1) * 128, :].astype(F32)
        scale = lax.rsqrt(jnp.sum(wide * wide, axis=-1, keepdims=True) + 1e-06)
        unit[c * 128 : (c + 1) * 128, :] = (wide * scale).astype(BF16)

    field = iota((META, ROWS), 0) // 16
    value = jnp.where(field == 0, member + 1, hops)
    value = jnp.where(field == 2, rank % 256, value)
    value = jnp.where(field == 3, (rank // 256) % 256, value)
    value = jnp.where(field == 4, rank // 65536, value)
    value = jnp.where((iota((META, ROWS), 0) % 16 == slot) & (field < 5), value, 0)
    meta = dot_nt(flag(which == target), value.astype(F32).astype(BF16))
    left[pl.ds(6, N, stride=8), :] = meta
    right[pl.ds(6, N, stride=8), :] = jnp.broadcast_to(jnp.minimum(queue[:1], 255.0), (N, 128))
    left[pl.ds(7, N, stride=8), :] = jnp.zeros((N, 128), F32)
    right[pl.ds(7, N, stride=8), :] = jnp.zeros((N, 128), F32)
    extra_row = jnp.where(slot >= 8, (slot - 8) * N + target, -1)
    late = dot(flag(iota((EXTRA, ROWS), 0) == extra_row), unit[...])
    for k in range(2):
        for piece in range(3):
            rows = late[k * N : (k + 1) * N, piece * 256 : (piece + 1) * 256]
            left[pl.ds(2 * piece + k, N, stride=8), :] = rows[:, :128]
            right[pl.ds(2 * piece + k, N, stride=8), :] = rows[:, 128:]
    out_ref[:, D : D + 128] = left[...].astype(BF16)
    out_ref[:, D + 128 :] = right[...].astype(BF16)

    main_row = jnp.where(slot < 8, target * 8 + slot, -1)
    for b in range(4):
        chosen = flag(iota((256, ROWS), 0) + b * 256 == main_row)
        out_ref[b * 256 : (b + 1) * 256, :D] = dot(chosen, unit[...]).astype(BF16)


def pack(emb, cluster, rank):
    return pl.pallas_call(
        pack_kernel,
        out_shape=(
            jax.ShapeDtypeStruct((MAIN, D + 256), BF16),
            jax.ShapeDtypeStruct((2, ROWS), I32),
        ),
        scratch_shapes=[
            pltpu.VMEM((ROWS, D), BF16),
            pltpu.VMEM((MAIN, 128), F32),
            pltpu.VMEM((MAIN, 128), F32),
        ],
        compiler_params=LIMIT,
        name="pack",
    )(emb, cluster.reshape(1, ROWS), rank.reshape(1, ROWS))


def unpack_kernel(
    got_ref, late_ref, column_ref, row_ref, near_ref, far_ref, bad_ref, left, right
):
    left[...] = got_ref[:, D : D + 128].astype(F32)
    right[...] = got_ref[:, D + 128 :].astype(F32)
    for k in range(2):
        for piece in range(3):
            for half, ref in enumerate((left, right)):
                at = piece * 256 + half * 128
                late_ref[k * N : (k + 1) * N, at : at + 128] = ref[
                    pl.ds(2 * piece + k, N, stride=8), :
                ].astype(BF16)
    meta = left[pl.ds(6, N, stride=8), :]
    queue = right[pl.ds(6, N, stride=8), :]
    meta_b = meta.astype(BF16)

    over_near = jnp.sum(jnp.minimum(queue, float(SLOTS)), axis=0, keepdims=True) - NEAR
    over_far = (
        jnp.sum(jnp.clip(queue - SLOTS, 0.0, float(SLOTS)), axis=0, keepdims=True) - FAR
    )
    over_long = jnp.max(queue, axis=0, keepdims=True) - 2.0 * SLOTS
    bad_ref[0, 0] = (
        jnp.max(jnp.maximum(jnp.maximum(over_near, over_far), over_long)) > 0.0
    ).astype(I32)

    spread = dot(flag(iota((MAIN, N), 0) // 8 == iota((MAIN, N), 1)), meta_b)
    spread = jnp.where(iota((MAIN, N), 1) % 16 == iota((MAIN, N), 0) % 8, spread, 0.0)
    lane = iota((N, N), 1)
    own = jnp.concatenate(
        [spread, jnp.where(lane % 16 == 8, meta, 0.0), jnp.where(lane % 16 == 9, meta, 0.0)],
        axis=0,
    ).astype(BF16)

    def weights(rows, shape, dim):
        field = iota(shape, dim) // 16
        weight = jnp.zeros(shape, F32)
        for at, by in rows:
            weight = jnp.where(field == at, by, weight)
        return weight.astype(BF16)

    rank_weights = ((2, 1.0), (3, 256.0), (4, 65536.0))
    cluster_weights = ((0, 1.0), (1, -16.0))
    column_ref[...] = dot(
        own,
        jnp.concatenate(
            [weights(rank_weights, (N, N), 0), weights(cluster_weights, (N, N), 0)], axis=1
        ),
    )
    row_ref[0:8, :] = dot_nt(weights(rank_weights, (8, N), 1), own)
    row_ref[8:16, :] = dot_nt(weights(cluster_weights, (8, N), 1), own)

    hops = pltpu.roll(meta, N - 16, 1)
    lower = flag(iota((N, N), 0) <= iota((N, N), 1))
    earlier = flag(iota((N, N), 0) > iota((N, N), 1))
    ones = jnp.ones((N, N), BF16)
    slot_of = iota((N, ALL), 1)
    slot_of = jnp.where(slot_of < MAIN, slot_of % 8, 8 + (slot_of - MAIN) // N)
    pick = flag(iota((N, ALL), 0) == slot_of)
    source_of = iota((N, ALL), 1)
    source_of = jnp.where(source_of < MAIN, source_of // 8, (source_of - MAIN) % N)
    of_source = iota((N, ALL), 0) == source_of

    field_lane = iota((N, N), 1)
    into = jnp.zeros((N, N), F32)
    for field, at in ((0, 2), (2, 3), (3, 4), (4, 5)):
        into = jnp.where((iota((N, N), 0) // 16 == field) & (field_lane == at), 1.0, into)
    card = dot(own, into.astype(BF16))
    line = iota((ALL, N), 0)
    card_lane = iota((ALL, N), 1)
    card = jnp.where(
        card_lane == 0, jnp.where(line < MAIN, line // 8, (line - MAIN) % N).astype(F32), card
    )
    card = jnp.where(
        card_lane == 1, jnp.where(line < MAIN, line % 8, 8 + (line - MAIN) // N).astype(F32), card
    )
    card = card.astype(BF16)

    for far, ref, length in ((1, near_ref, NEAR), (2, far_ref, FAR)):
        moves = (lane < SLOTS) & (meta > 0.0) & (hops == float(far))
        moves_b = flag(moves)
        number = dot(moves_b, lower) + dot(earlier, dot(moves_b, ones).astype(BF16))
        number = jnp.where(moves, number, 0.0).astype(BF16)
        number = jnp.sum(jnp.where(of_source, dot(number, pick), 0.0), axis=0, keepdims=True)
        chosen = flag(iota((length, ALL), 0) + 1 == number.astype(I32))
        sent = dot(chosen[:, :MAIN], got_ref[:, :D]) + dot(chosen[:, MAIN:], late_ref[...])
        ref[:, :D] = sent.astype(BF16)
        ref[:, D:] = dot(chosen, card).astype(BF16)


def unpack(got):
    return pl.pallas_call(
        unpack_kernel,
        out_shape=(
            jax.ShapeDtypeStruct((EXTRA, D), BF16),
            jax.ShapeDtypeStruct((ALL, 256), F32),
            jax.ShapeDtypeStruct((16, ALL), F32),
            jax.ShapeDtypeStruct((NEAR, D + META), BF16),
            jax.ShapeDtypeStruct((FAR, D + META), BF16),
            jax.ShapeDtypeStruct((1, 1), I32),
        ),
        out_specs=(pl.BlockSpec(memory_space=pltpu.VMEM),) * 5
        + (pl.BlockSpec(memory_space=pltpu.SMEM),),
        scratch_shapes=[pltpu.VMEM((MAIN, 128), F32), pltpu.VMEM((MAIN, 128), F32)],
        compiler_params=LIMIT,
        name="unpack",
    )(got)


def local_kernel(got_ref, late_ref, column_ref, row_ref, best_ref):
    best_ref[...] = jnp.full((8, ALL), -1.0, F32)

    def rows_of(b):
        if b * 256 < MAIN:
            return got_ref[b * 256 : (b + 1) * 256, :D]
        return late_ref[...]

    blocks = ALL // 256
    for i in range(blocks):
        rank = column_ref[i * 256 : (i + 1) * 256, :128]
        cluster = column_ref[i * 256 : (i + 1) * 256, 128:]
        rank = jnp.concatenate([rank, rank], axis=1)
        cluster = jnp.concatenate([cluster, cluster], axis=1)
        for j in range(blocks):
            across = slice(j * 256, (j + 1) * 256)
            similar = dot_nt(rows_of(i), rows_of(j))
            earlier = (cluster == row_ref[8:9, across]) & (rank < row_ref[0:1, across])
            kept = jnp.where(earlier, similar, -1.0)
            best_ref[:, across] = jnp.maximum(
                best_ref[:, across], jnp.max(kept.reshape(32, 8, 256), axis=0)
            )


def local_best(got, late, column, row):
    return pl.pallas_call(
        local_kernel,
        out_shape=jax.ShapeDtypeStruct((8, ALL), F32),
        compiler_params=LIMIT,
        cost_estimate=pl.CostEstimate(
            flops=2 * ALL * ALL * D, bytes_accessed=4 * ALL * D, transcendentals=0
        ),
        name="local_best",
    )(got, late, column, row)


def cross_kernel(got_ref, late_ref, row_ref, best_ref, near_ref, far_ref, out_ref, moved):
    moved[0:NEAR, :] = near_ref[...]
    moved[NEAR : NEAR + FAR, :] = far_ref[...]
    moved[NEAR + FAR :, :] = jnp.zeros((MOVED - NEAR - FAR, D + META), BF16)
    card = moved[:, D:]

    def weigh(rows, shape, dim):
        at = iota(shape, dim)
        weight = jnp.zeros(shape, F32)
        for lane, by in rows:
            weight = jnp.where(at == lane, by, weight)
        return weight.astype(BF16)

    rank_weights = ((3, 1.0), (4, 256.0), (5, 65536.0))
    column = dot(
        card,
        jnp.concatenate(
            [
                weigh(rank_weights, (META, 128), 0),
                weigh(((2, 1.0),), (META, 128), 0),
                weigh(((0, 1.0),), (META, 128), 0),
                weigh(((1, 1.0),), (META, 128), 0),
            ],
            axis=1,
        ),
    )
    rank, cluster = column[:, :128], column[:, 128:256]
    source, slot = column[:, 256:384], column[:, 384:]
    moved_rank = dot_nt(weigh(rank_weights, (8, META), 1), card)
    moved_cluster = dot_nt(weigh(((2, 1.0),), (8, META), 1), card)
    rank2 = jnp.concatenate([rank, rank], axis=1)
    cluster2 = jnp.concatenate([cluster, cluster], axis=1)

    unit = moved[:, :D]
    arrived = jnp.full((MOVED, 256), -1.0, F32)
    bests = []
    for j in range(ALL // 256):
        across = slice(j * 256, (j + 1) * 256)
        rows = got_ref[across, :D] if j * 256 < MAIN else late_ref[...]
        similar = dot_nt(unit, rows)
        same = cluster2 == row_ref[8:9, across]
        earlier = rank2 < row_ref[0:1, across]
        kept = jnp.where(same & earlier, similar, -1.0)
        here = jnp.maximum(best_ref[:, across], jnp.max(kept.reshape(32, 8, 256), axis=0))
        bests.append(jnp.max(here, axis=0, keepdims=True))
        later = rank2 > row_ref[0:1, across]
        arrived = jnp.maximum(arrived, jnp.where(same & later, similar, -1.0))
    similar = dot_nt(unit, unit)
    later = (cluster2 == moved_cluster[:1]) & (rank2 > moved_rank[:1])
    arrived = jnp.maximum(arrived, jnp.where(later, similar, -1.0))
    arrived = jnp.max(arrived, axis=1, keepdims=True)

    row_of = iota((N, MAIN), 0) == iota((N, MAIN), 1) // 8
    main = jnp.concatenate(bests[: MAIN // 256], axis=1)
    main = jnp.where(row_of, main, 0.0)
    out = dot(main, flag(iota((MAIN, N), 0) % 8 == iota((MAIN, N), 1), F32), HIGHEST)
    for k in range(2):
        late = bests[MAIN // 256][:, k * N : (k + 1) * N]
        late = jnp.where(iota((N, N), 0) == iota((N, N), 1), late, 0.0)
        out = out + dot(late, flag(iota((N, N), 1) == 8 + k, F32), HIGHEST)
    hop = jnp.where(iota((MOVED, N), 0) < NEAR, 1, 2)
    answers = jnp.where(
        (cluster > 0.0) & (iota((MOVED, N), 1) == hop * 16 + slot.astype(I32)), arrived, 0.0
    )
    sender = flag((cluster > 0.0) & (iota((MOVED, N), 1) == source.astype(I32)), F32)
    out = out + dot(sender.T, answers, HIGHEST)
    out_ref[...] = out


def cross_best(got, late, row, best, near, far):
    return pl.pallas_call(
        cross_kernel,
        out_shape=jax.ShapeDtypeStruct((N, N), F32),
        scratch_shapes=[pltpu.VMEM((MOVED, D + META), BF16)],
        compiler_params=LIMIT,
        name="cross_best",
    )(got, late, row, best, near, far)


def pick_kernel(back_ref, place_ref, out_ref):
    home = place_ref[0:1, :]
    lane = place_ref[1:2, :]
    table = dot(back_ref[...].T, flag(iota((N, ROWS), 0) == home, F32), HIGHEST)
    out_ref[...] = jnp.sum(
        jnp.where(iota((N, ROWS), 0) == lane, table, 0.0), axis=0, keepdims=True
    )


def pick(back, place):
    return pl.pallas_call(
        pick_kernel,
        out_shape=jax.ShapeDtypeStruct((1, ROWS), F32),
        compiler_params=LIMIT,
        name="pick",
    )(back, place)


def passed_along(array, by):
    return lax.ppermute(array, "dev", [(i, (i + by) % N) for i in range(N)])


def swapped(array):
    return lax.all_to_all(array, "dev", split_axis=0, concat_axis=0, tiled=True)


def paired_best(left, right):
    left_unit, left_cluster, left_rank = left
    right_unit, right_cluster, right_rank = right
    block_rows = 512
    block_count = left_unit.shape[0] // block_rows
    blocked = (
        left_unit.reshape(block_count, block_rows, D),
        left_cluster.reshape(block_count, block_rows),
        left_rank.reshape(block_count, block_rows),
    )

    def advance(carry, pieces):
        unit, cluster, rank = pieces
        similar = dot_nt(unit, right_unit)
        same = (cluster[:, None] == right_cluster[None, :]) & (right_cluster[None, :] >= 0)
        earlier = same & (right_rank[None, :] < rank[:, None])
        return carry, jnp.max(jnp.where(earlier, similar, -1.0), axis=1)

    return lax.scan(advance, 0, blocked)[1].reshape(-1)


def by_pools(emb, cluster, rank):
    capacity = 2 * ROWS // N
    pool_rows = N * capacity
    wide = emb.astype(F32)
    unit = (wide * lax.rsqrt(jnp.sum(wide * wide, axis=-1, keepdims=True) + 1e-06)).astype(BF16)
    target = (cluster % N + rank % 2) % N
    one_hot = (target[:, None] == jnp.arange(N, dtype=I32)[None, :]).astype(I32)
    slot = jnp.sum(jnp.cumsum(one_hot, axis=0) * one_hot, axis=1) - 1
    placing = target * capacity + slot
    received = (
        swapped(jnp.zeros((pool_rows, D), BF16).at[placing].set(unit)),
        swapped(jnp.full((pool_rows,), -1, I32).at[placing].set(cluster)),
        swapped(jnp.zeros((pool_rows,), I32).at[placing].set(rank)),
    )
    best = paired_best(received, received)
    for by in (1, -1):
        other = tuple(passed_along(part, by) for part in received)
        best = jnp.maximum(best, paired_best(received, other))
    return swapped(best)[placing]


def per_device(emb, cluster, rank):
    packed, place = pack(emb, cluster, rank)
    got = swapped(packed.reshape(N, 8, D + 256)).reshape(MAIN, D + 256)
    late, column, row, near, far, bad = unpack(got)
    near = passed_along(near, -1)
    far = passed_along(far, -2)
    best = local_best(got, late, column, row)
    answers = cross_best(got, late, row, best, near, far)
    back = swapped(answers.reshape(N, 1, N)).reshape(N, N)
    nearest = pick(back, place).reshape(ROWS)
    return lax.cond(
        bad[0, 0] > 0,
        by_pools,
        lambda emb, cluster, rank: nearest,
        emb,
        cluster,
        rank,
    )


def solution(mesh):
    placed = (P("dev", None), P("dev"), P("dev"))
    return jax.shard_map(
        per_device, mesh=mesh, in_specs=placed, out_specs=P("dev"), check_vma=False
    )
```

```python
import functools

import jax
import jax.numpy as jnp
from jax import lax
from jax.experimental import pallas as pl
from jax.experimental.pallas import tpu as pltpu
from jax.sharding import PartitionSpec as P

F32 = jnp.float32
BF16 = jnp.bfloat16
I32 = jnp.int32

N = 128
ROWS = 1024
D = 768
SLOTS = 10
MAIN = 8 * N
EXTRA = 2 * N
ALL = MAIN + EXTRA
NEAR = 144
FAR = 16
MOVED = NEAR + FAR
META = 128
LIMIT = pltpu.CompilerParams(vmem_limit_bytes=20 * 1024 * 1024)


def iota(shape, dim):
    return lax.broadcasted_iota(I32, shape, dim)


def flag(mask, dtype=BF16):
    return jnp.where(mask, 1.0, 0.0).astype(dtype)


def dot(a, b):
    return jnp.dot(a, b, preferred_element_type=F32)


def dot_nt(a, b):
    return lax.dot_general(a, b, (((1,), (1,)), ((), ())), preferred_element_type=F32)


def parts(a):
    high = a.astype(BF16)
    rest = a - high.astype(F32)
    middle = rest.astype(BF16)
    return high, middle, (rest - middle.astype(F32)).astype(BF16)


def weights(rows, shape, dim, size=16):
    group = iota(shape, dim) // size
    weight = jnp.zeros(shape, F32)
    for at, by in rows:
        weight = jnp.where(group == at, by, weight)
    return weight.astype(BF16)


def pack_kernel(
    emb_ref, cluster_ref, rank_ref, out_ref, place_ref, raw, unit, left, right, arrived
):
    loads = [
        pltpu.make_async_copy(
            emb_ref.at[pl.ds(c * 256, 256), :], raw.at[pl.ds(c * 256, 256), :], arrived.at[c]
        )
        for c in range(4)
    ]
    for load in loads:
        load.start()

    cluster = cluster_ref[...]
    rank = rank_ref[...]
    home = cluster & (N - 1)
    member = cluster // N

    which = iota((N, ROWS), 0)
    at_home = which == home
    at_home_b = flag(at_home)
    count = dot_nt(jnp.ones((8, ROWS), BF16), at_home_b)
    chunks = jnp.concatenate([at_home_b[:, c * 128 : (c + 1) * 128] for c in range(8)], axis=0)
    lower = flag(iota((128, 128), 0) <= iota((128, 128), 1))
    running = dot(chunks, jnp.concatenate([lower, jnp.ones((128, 128), BF16)], axis=1))

    window = count - float(SLOTS)
    queue = jnp.maximum(window, 0.0)
    for step in (1, 2, 4, 8, 16, 32, 64):
        queue = jnp.maximum(queue, window + pltpu.roll(queue, step, 1))
        window = window + pltpu.roll(window, step, 1)
    ahead = pltpu.roll(queue, 1, 1)
    ahead_high = jnp.floor(ahead * (1.0 / 256.0)) * 256.0
    ahead = dot(jnp.concatenate([ahead_high, ahead - ahead_high], axis=0).astype(BF16), at_home_b)
    ahead = ahead[0:1] + ahead[8:9]

    before = jnp.zeros((128, 128), F32)
    turn = []
    for c in range(8):
        part = running[c * 128 : (c + 1) * 128]
        turn.append(
            jnp.sum(
                jnp.where(at_home[:, c * 128 : (c + 1) * 128], part[:, :128] + before, 0.0),
                axis=0,
                keepdims=True,
            )
        )
        before = before + part[:, 128:]
    offset = jnp.concatenate(turn, axis=1) - 1.0 + ahead
    hops = jnp.floor((offset + 0.5) * (1.0 / SLOTS))
    slot = (offset - hops * SLOTS).astype(I32)
    hops = hops.astype(I32)
    target = (home + hops) & (N - 1)
    place_ref[0:1, :] = home
    place_ref[1:2, :] = jnp.minimum(hops, 7) * 16 + slot

    for c in range(4):
        loads[c].wait()
        wide = raw[c * 256 : (c + 1) * 256, :].astype(F32)
        scale = lax.rsqrt(jnp.sum(wide * wide, axis=-1, keepdims=True) + 1e-06)
        unit[c * 256 : (c + 1) * 256, :] = (wide * scale).astype(BF16)

    def spread(value):
        return jnp.broadcast_to(value, (16, ROWS))

    value = jnp.concatenate(
        [
            spread(member + 1),
            spread(hops),
            spread(rank & 255),
            spread((rank >> 8) & 255),
            spread(rank >> 16),
            jnp.zeros((48, ROWS), I32),
        ],
        axis=0,
    )
    value = jnp.where((iota((META, ROWS), 0) & 15) == slot, value, 0)
    meta = dot_nt(flag(which == target), value.astype(F32).astype(BF16))
    left[pl.ds(6, N, stride=8), :] = meta
    right[pl.ds(6, N, stride=8), :] = jnp.broadcast_to(jnp.minimum(queue[:1], 255.0), (N, 128))
    left[pl.ds(7, N, stride=8), :] = jnp.zeros((N, 128), F32)
    right[pl.ds(7, N, stride=8), :] = jnp.zeros((N, 128), F32)
    extra_row = jnp.where(slot >= 8, (slot - 8) * N + target, -1)
    late = dot(flag(iota((EXTRA, ROWS), 0) == extra_row), unit[...])
    for k in range(2):
        for piece in range(3):
            rows = late[k * N : (k + 1) * N, piece * 256 : (piece + 1) * 256]
            left[pl.ds(2 * piece + k, N, stride=8), :] = rows[:, :128]
            right[pl.ds(2 * piece + k, N, stride=8), :] = rows[:, 128:]
    out_ref[:, D : D + 128] = left[...].astype(BF16)
    out_ref[:, D + 128 :] = right[...].astype(BF16)

    main_row = jnp.where(slot < 8, target * 8 + slot, -1)
    for b in range(4):
        chosen = flag(iota((256, ROWS), 0) == main_row - b * 256)
        out_ref[b * 256 : (b + 1) * 256, :D] = dot(chosen, unit[...]).astype(BF16)


def pack(emb, cluster, rank):
    return pl.pallas_call(
        pack_kernel,
        in_specs=[
            pl.BlockSpec(memory_space=pl.ANY),
            pl.BlockSpec(memory_space=pltpu.VMEM),
            pl.BlockSpec(memory_space=pltpu.VMEM),
        ],
        out_shape=(
            jax.ShapeDtypeStruct((MAIN, D + 256), BF16),
            jax.ShapeDtypeStruct((2, ROWS), I32),
        ),
        scratch_shapes=[
            pltpu.VMEM((ROWS, D), BF16),
            pltpu.VMEM((ROWS, D), BF16),
            pltpu.VMEM((MAIN, 128), F32),
            pltpu.VMEM((MAIN, 128), F32),
            pltpu.SemaphoreType.DMA((4,)),
        ],
        compiler_params=LIMIT,
        name="pack",
    )(emb, cluster.reshape(1, ROWS), rank.reshape(1, ROWS))


def unpack_kernel(got_ref, late_ref, meta_ref, near_ref, far_ref, bad_ref, left, right):
    left[...] = got_ref[:, D : D + 128].astype(F32)
    right[...] = got_ref[:, D + 128 :].astype(F32)
    for k in range(2):
        for piece in range(3):
            for half, ref in enumerate((left, right)):
                at = piece * 256 + half * 128
                late_ref[k * N : (k + 1) * N, at : at + 128] = ref[
                    pl.ds(2 * piece + k, N, stride=8), :
                ].astype(BF16)
    meta = left[pl.ds(6, N, stride=8), :]
    queue = right[pl.ds(6, N, stride=8), :]
    meta_ref[...] = meta

    over_near = jnp.sum(jnp.minimum(queue, float(SLOTS)), axis=0, keepdims=True) - NEAR
    over_far = (
        jnp.sum(jnp.clip(queue - SLOTS, 0.0, float(SLOTS)), axis=0, keepdims=True) - FAR
    )
    over_long = jnp.max(queue, axis=0, keepdims=True) - 2.0 * SLOTS
    bad_ref[0, 0] = (
        jnp.max(jnp.maximum(jnp.maximum(over_near, over_far), over_long)) > 0.0
    ).astype(I32)

    lane = iota((N, N), 1)
    hops = pltpu.roll(meta, N - 16, 1)
    moves = (lane < SLOTS) & (meta > 0.0)
    one = flag(moves & (hops == 1.0))
    two = flag(moves & (hops == 2.0))
    each = dot_nt(jnp.ones((8, N), BF16), jnp.concatenate([one, two], axis=0))
    first = dot(
        jnp.concatenate([each[:, :N], each[:, N:]], axis=0).astype(BF16),
        flag(iota((N, N), 0) < iota((N, N), 1)),
    )
    count_one, count_two = each[0:1, :N], each[0:1, N:]
    first_one, first_two = first[0:1], first[8:9]

    def rows_of(length, first, count, skip):
        line = iota((length, N), 0).astype(F32)
        mine = (line >= first) & (line < first + count)
        source = jnp.sum(jnp.where(mine, iota((length, N), 1).astype(F32), 0.0), 1, keepdims=True)
        place = jnp.sum(jnp.where(mine, line - first + skip, 0.0), 1, keepdims=True)
        any_row = line[:, :1] < jnp.sum(count, 1, keepdims=True)
        return flag(mine), source.astype(I32), place.astype(I32), any_row

    near = rows_of(NEAR, first_one, count_one, count_two)
    far = rows_of(FAR, first_two, count_two, 0.0)
    mine, source, slot = (jnp.concatenate([a, b], axis=0) for a, b in zip(near[:3], far[:3]))
    used = jnp.concatenate([near[3].astype(I32), far[3].astype(I32)], axis=0) > 0

    at_main = jnp.where(used & (slot < 8), source * 8 + slot, -1)
    at_late = jnp.where(used & (slot >= 8), (slot - 8) * N + source, -1)
    sent = dot(flag(iota((MOVED, MAIN), 1) == at_main), got_ref[:, :D]) + dot(
        flag(iota((MOVED, EXTRA), 1) == at_late), late_ref[...]
    )
    sent = sent.astype(BF16)
    card = dot(mine, meta.astype(BF16))
    lanes = iota((MOVED, META), 1)
    card = jnp.where((lanes & 15) == slot, card, 0.0)
    card = jnp.where(lanes == 96, source.astype(F32), card)
    card = jnp.where(lanes == 97, slot.astype(F32), card).astype(BF16)
    near_ref[:, :D] = sent[:NEAR]
    near_ref[:, D:] = card[:NEAR]
    far_ref[:, :D] = sent[NEAR:]
    far_ref[:, D:] = card[NEAR:]


def unpack(got):
    return pl.pallas_call(
        unpack_kernel,
        out_shape=(
            jax.ShapeDtypeStruct((EXTRA, D), BF16),
            jax.ShapeDtypeStruct((N, META), F32),
            jax.ShapeDtypeStruct((NEAR, D + META), BF16),
            jax.ShapeDtypeStruct((FAR, D + META), BF16),
            jax.ShapeDtypeStruct((1, 1), I32),
        ),
        out_specs=(pl.BlockSpec(memory_space=pltpu.VMEM),) * 4
        + (pl.BlockSpec(memory_space=pltpu.SMEM),),
        scratch_shapes=[pltpu.VMEM((MAIN, 128), F32), pltpu.VMEM((MAIN, 128), F32)],
        compiler_params=LIMIT,
        name="unpack",
    )(got)


RANK = ((2, 1.0), (3, 256.0), (4, 65536.0))
CLUSTER = ((0, 1.0), (1, -16.0))


def local_kernel(got_ref, late_ref, meta_ref, row_ref, best_ref, own, column):
    meta = meta_ref[...]
    spread = dot(flag((iota((MAIN, N), 0) >> 3) == iota((MAIN, N), 1)), meta.astype(BF16))
    own[:MAIN, :] = jnp.where(
        (iota((MAIN, N), 1) & 15) == (iota((MAIN, N), 0) & 7), spread, 0.0
    ).astype(BF16)
    lane = iota((N, N), 1) & 15
    for k in range(2):
        own[MAIN + k * N : MAIN + (k + 1) * N, :] = jnp.where(lane == 8 + k, meta, 0.0).astype(BF16)
    row_ref[...] = dot_nt(
        jnp.concatenate([weights(RANK, (8, N), 1), weights(CLUSTER, (8, N), 1)], axis=0), own[...]
    )
    column[...] = dot(
        own[...],
        jnp.concatenate([weights(RANK, (N, N), 0), weights(CLUSTER, (N, N), 0)], axis=1),
    )
    best_ref[...] = jnp.full((8, ALL), -1.0, F32)

    def rows_of(b):
        if b * 256 < MAIN:
            return got_ref[b * 256 : (b + 1) * 256, :D]
        return late_ref[...]

    blocks = ALL // 256
    for i in range(blocks):
        rank = column[i * 256 : (i + 1) * 256, :128]
        cluster = column[i * 256 : (i + 1) * 256, 128:]
        rank = jnp.concatenate([rank, rank], axis=1)
        cluster = jnp.concatenate([cluster, cluster], axis=1)
        for j in range(blocks):
            across = slice(j * 256, (j + 1) * 256)
            similar = dot_nt(rows_of(i), rows_of(j))
            earlier = (cluster == row_ref[8:9, across]) & (rank < row_ref[0:1, across])
            kept = jnp.where(earlier, similar, -1.0)
            best_ref[:, across] = jnp.maximum(
                best_ref[:, across], jnp.max(kept.reshape(32, 8, 256), axis=0)
            )


def local_best(got, late, meta):
    return pl.pallas_call(
        local_kernel,
        out_shape=(
            jax.ShapeDtypeStruct((16, ALL), F32),
            jax.ShapeDtypeStruct((8, ALL), F32),
        ),
        scratch_shapes=[pltpu.VMEM((ALL, N), BF16), pltpu.VMEM((ALL, 256), F32)],
        compiler_params=LIMIT,
        cost_estimate=pl.CostEstimate(
            flops=2 * ALL * ALL * D, bytes_accessed=4 * ALL * D, transcendentals=0
        ),
        name="local_best",
    )(got, late, meta)


def cross_kernel(got_ref, late_ref, row_ref, best_ref, near_ref, far_ref, out_ref, moved):
    moved[0:NEAR, :] = near_ref[...]
    moved[NEAR:, :] = far_ref[...]
    card = moved[:, D:]
    column = dot(
        card,
        jnp.concatenate(
            [
                weights(RANK, (META, 128), 0),
                weights(CLUSTER[:1], (META, 128), 0),
                weights(((96, 1.0),), (META, 128), 0, 1),
                weights(((97, 1.0),), (META, 128), 0, 1),
            ],
            axis=1,
        ),
    )
    rank, cluster = column[:, :128], column[:, 128:256]
    source, slot = column[:, 256:384].astype(I32), column[:, 384:].astype(I32)
    moved_row = dot_nt(
        jnp.concatenate([weights(RANK, (8, META), 1), weights(CLUSTER[:1], (8, META), 1)], axis=0),
        card,
    )
    rank2 = jnp.concatenate([rank, rank], axis=1)
    cluster2 = jnp.concatenate([cluster, cluster], axis=1)

    unit = moved[:, :D]
    arrived = jnp.full((MOVED, 256), -1.0, F32)
    bests = []
    for j in range(ALL // 256):
        across = slice(j * 256, (j + 1) * 256)
        rows = got_ref[across, :D] if j * 256 < MAIN else late_ref[...]
        similar = dot_nt(unit, rows)
        same = cluster2 == row_ref[8:9, across]
        earlier = rank2 < row_ref[0:1, across]
        kept = jnp.where(same & earlier, similar, -1.0)
        here = jnp.maximum(best_ref[:, across], jnp.max(kept.reshape(MOVED // 8, 8, 256), axis=0))
        bests.append(jnp.max(here, axis=0, keepdims=True))
        later = rank2 > row_ref[0:1, across]
        arrived = jnp.maximum(arrived, jnp.where(same & later, similar, -1.0))
    similar = dot_nt(unit, unit)
    later = (cluster2[:, :MOVED] == moved_row[8:9]) & (rank2[:, :MOVED] > moved_row[0:1])
    arrived = jnp.maximum(
        jnp.max(arrived, axis=1, keepdims=True),
        jnp.max(jnp.where(later, similar, -1.0), axis=1, keepdims=True),
    )

    main = jnp.concatenate(bests[: MAIN // 256], axis=1)
    main = jnp.where((iota((8, MAIN), 1) & 7) == iota((8, MAIN), 0), main, 0.0)
    of_sender = flag((iota((MAIN, N), 0) >> 3) == iota((MAIN, N), 1))
    answers = sum(dot(part, of_sender) for part in parts(main))
    late = bests[MAIN // 256]
    answers = jnp.concatenate(
        [answers, late[:, :N], late[:, N:], jnp.zeros((N - SLOTS, N), F32)], axis=0
    )
    hop = jnp.where(iota((MOVED, N), 0) < NEAR, 16, 32)
    by_lane = jnp.where((cluster > 0.0) & (iota((MOVED, N), 1) == hop + slot), arrived, 0.0)
    sender = flag((cluster > 0.0) & (iota((MOVED, N), 1) == source), F32).T.astype(BF16)
    out_ref[...] = answers.T + sum(dot(sender, part) for part in parts(by_lane))


def cross_best(got, late, row, best, near, far):
    return pl.pallas_call(
        cross_kernel,
        out_shape=jax.ShapeDtypeStruct((N, N), F32),
        scratch_shapes=[pltpu.VMEM((MOVED, D + META), BF16)],
        compiler_params=LIMIT,
        name="cross_best",
    )(got, late, row, best, near, far)


def pick_kernel(back_ref, place_ref, out_ref):
    home = place_ref[0:1, :]
    lane = place_ref[1:2, :]
    at_home = flag(iota((N, ROWS), 0) == home)
    table = sum(dot(part, at_home) for part in parts(back_ref[...].T[:48]))
    out_ref[...] = jnp.sum(
        jnp.where(iota((48, ROWS), 0) == lane, table, 0.0), axis=0, keepdims=True
    )


def pick(back, place):
    return pl.pallas_call(
        pick_kernel,
        out_shape=jax.ShapeDtypeStruct((1, ROWS), F32),
        compiler_params=LIMIT,
        name="pick",
    )(back, place)


def passed_along(array, by):
    return lax.ppermute(array, "dev", [(i, (i + by) % N) for i in range(N)])


def swapped(array):
    return lax.all_to_all(array, "dev", split_axis=0, concat_axis=0, tiled=True)


def paired_best(left, right):
    left_unit, left_cluster, left_rank = left
    right_unit, right_cluster, right_rank = right
    block_rows = 512
    block_count = left_unit.shape[0] // block_rows
    blocked = (
        left_unit.reshape(block_count, block_rows, D),
        left_cluster.reshape(block_count, block_rows),
        left_rank.reshape(block_count, block_rows),
    )

    def advance(carry, pieces):
        unit, cluster, rank = pieces
        similar = dot_nt(unit, right_unit)
        same = (cluster[:, None] == right_cluster[None, :]) & (right_cluster[None, :] >= 0)
        earlier = same & (right_rank[None, :] < rank[:, None])
        return carry, jnp.max(jnp.where(earlier, similar, -1.0), axis=1)

    return lax.scan(advance, 0, blocked)[1].reshape(-1)


def by_pools(emb, cluster, rank):
    capacity = 2 * ROWS // N
    pool_rows = N * capacity
    wide = emb.astype(F32)
    unit = (wide * lax.rsqrt(jnp.sum(wide * wide, axis=-1, keepdims=True) + 1e-06)).astype(BF16)
    target = (cluster % N + rank % 2) % N
    one_hot = (target[:, None] == jnp.arange(N, dtype=I32)[None, :]).astype(I32)
    slot = jnp.sum(jnp.cumsum(one_hot, axis=0) * one_hot, axis=1) - 1
    placing = target * capacity + slot
    received = (
        swapped(jnp.zeros((pool_rows, D), BF16).at[placing].set(unit)),
        swapped(jnp.full((pool_rows,), -1, I32).at[placing].set(cluster)),
        swapped(jnp.zeros((pool_rows,), I32).at[placing].set(rank)),
    )
    best = paired_best(received, received)
    for by in (1, -1):
        other = tuple(passed_along(part, by) for part in received)
        best = jnp.maximum(best, paired_best(received, other))
    return swapped(best)[placing]


def per_device(emb, cluster, rank):
    packed, place = pack(emb, cluster, rank)
    got = swapped(packed.reshape(N, 8, D + 256)).reshape(MAIN, D + 256)
    late, meta, near, far, bad = unpack(got)
    near = passed_along(near, -1)
    far = passed_along(far, -2)
    row, best = local_best(got, late, meta)
    answers = cross_best(got, late, row, best, near, far)
    back = swapped(answers.reshape(N, 1, N)).reshape(N, N)
    nearest = pick(back, place).reshape(ROWS)
    return lax.cond(
        bad[0, 0] > 0,
        by_pools,
        lambda emb, cluster, rank: nearest,
        emb,
        cluster,
        rank,
    )


def solution(mesh):
    placed = (P("dev", None), P("dev"), P("dev"))
    return jax.shard_map(
        per_device, mesh=mesh, in_specs=placed, out_specs=P("dev"), check_vma=False
    )
```

```python
import functools

import jax
import jax.numpy as jnp
from jax import lax
from jax.experimental import pallas as pl
from jax.experimental.pallas import tpu as pltpu
from jax.sharding import PartitionSpec as P

F32 = jnp.float32
BF16 = jnp.bfloat16
I32 = jnp.int32

N = 128
ROWS = 1024
D = 768
SLOTS = 10
MAIN = 8 * N
EXTRA = 2 * N
ALL = MAIN + EXTRA
NEAR = 144
FAR = 16
MOVED = NEAR + FAR
META = 128
LIMIT = pltpu.CompilerParams(vmem_limit_bytes=20 * 1024 * 1024)


def iota(shape, dim):
    return lax.broadcasted_iota(I32, shape, dim)


def flag(mask, dtype=BF16):
    return jnp.where(mask, 1.0, 0.0).astype(dtype)


def dot(a, b):
    return jnp.dot(a, b, preferred_element_type=F32)


def dot_nt(a, b):
    return lax.dot_general(a, b, (((1,), (1,)), ((), ())), preferred_element_type=F32)


def parts(a):
    high = a.astype(BF16)
    rest = a - high.astype(F32)
    middle = rest.astype(BF16)
    return high, middle, (rest - middle.astype(F32)).astype(BF16)


def weights(rows, shape, dim, size=16):
    group = iota(shape, dim) // size
    weight = jnp.zeros(shape, F32)
    for at, by in rows:
        weight = jnp.where(group == at, by, weight)
    return weight.astype(BF16)


RING_Y = 1878693120
RING_Z = 29252580


def device_at(turn):
    place = turn >> 3
    x = ((turn >> 1) & 3) ^ ((place & 1) * 3)
    y = (RING_Y >> (place * 2)) & 3
    z = (RING_Z >> (place * 2)) & 3
    return z * 32 + y * 8 + x * 2 + (turn & 1)


def pack_kernel(
    emb_ref, cluster_ref, rank_ref, out_ref, place_ref, raw, unit, left, right, arrived
):
    loads = [
        pltpu.make_async_copy(
            emb_ref.at[pl.ds(c * 256, 256), :], raw.at[pl.ds(c * 256, 256), :], arrived.at[c]
        )
        for c in range(4)
    ]
    for load in loads:
        load.start()

    cluster = cluster_ref[...]
    rank = rank_ref[...]
    home = cluster & (N - 1)
    member = cluster // N

    which = iota((N, ROWS), 0)
    at_home = which == home
    at_home_b = flag(at_home)
    row, column = iota((N, N), 0), iota((N, N), 1)
    upper = flag(row < column)
    count = dot_nt(jnp.ones((8, ROWS), BF16), at_home_b)
    chunks = jnp.concatenate([at_home_b[:, c * 128 : (c + 1) * 128] for c in range(8)], axis=0)
    running = dot(chunks, jnp.concatenate([upper, jnp.ones((N, N), BF16)], axis=1))
    totals = [running[c * 128 : (c + 1) * 128, 128:] for c in range(8)]
    total = sum(totals[1:], totals[0])

    over = total - float(SLOTS)
    below = dot(flag(row > column), over.astype(BF16))
    along = dot((count - float(SLOTS)).astype(BF16), upper)
    round_trip = float(ROWS - SLOTS * N)
    ahead = below + jnp.max(
        jnp.where(column < row, 0.0, round_trip) - along[:1], axis=1, keepdims=True
    )
    ahead = jnp.maximum(ahead, 0.0)
    queue = along[:1] + count[:1] - float(SLOTS)
    queue = queue + jnp.max(
        jnp.where(row <= column, 0.0, round_trip) - below, axis=0, keepdims=True
    )
    queue = jnp.maximum(queue, 0.0)

    before = ahead
    turn = []
    for c in range(8):
        part = running[c * 128 : (c + 1) * 128, :128]
        turn.append(
            jnp.sum(
                jnp.where(at_home[:, c * 128 : (c + 1) * 128], part + before, 0.0),
                axis=0,
                keepdims=True,
            )
        )
        before = before + totals[c]
    offset = jnp.concatenate(turn, axis=1)
    hops = jnp.floor((offset + 0.5) * (1.0 / SLOTS))
    slot = (offset - hops * SLOTS).astype(I32)
    hops = hops.astype(I32)
    target = device_at((home + hops) & (N - 1))
    place_ref[0:1, :] = device_at(home)
    place_ref[1:2, :] = jnp.minimum(hops, 7) * 16 + slot

    for c in range(4):
        loads[c].wait()
        wide = raw[c * 256 : (c + 1) * 256, :].astype(F32)
        scale = lax.rsqrt(jnp.sum(wide * wide, axis=-1, keepdims=True) + 1e-06)
        unit[c * 256 : (c + 1) * 256, :] = (wide * scale).astype(BF16)

    def spread(value):
        return jnp.broadcast_to(value, (16, ROWS))

    value = jnp.concatenate(
        [
            spread(member + 1),
            spread(hops),
            spread(rank & 255),
            spread((rank >> 8) & 255),
            spread(rank >> 16),
            jnp.zeros((48, ROWS), I32),
        ],
        axis=0,
    )
    value = jnp.where((iota((META, ROWS), 0) & 15) == slot, value, 0)
    meta = dot_nt(flag(which == target), value.astype(F32).astype(BF16))
    left[pl.ds(6, N, stride=8), :] = meta
    right[pl.ds(6, N, stride=8), :] = jnp.broadcast_to(jnp.minimum(queue, 255.0), (N, 128))
    left[pl.ds(7, N, stride=8), :] = jnp.zeros((N, 128), F32)
    right[pl.ds(7, N, stride=8), :] = jnp.zeros((N, 128), F32)
    extra_row = jnp.where(slot >= 8, (slot - 8) * N + target, -1)
    late = dot(flag(iota((EXTRA, ROWS), 0) == extra_row), unit[...])
    for k in range(2):
        for piece in range(3):
            rows = late[k * N : (k + 1) * N, piece * 256 : (piece + 1) * 256]
            left[pl.ds(2 * piece + k, N, stride=8), :] = rows[:, :128]
            right[pl.ds(2 * piece + k, N, stride=8), :] = rows[:, 128:]
    out_ref[:, D : D + 128] = left[...].astype(BF16)
    out_ref[:, D + 128 :] = right[...].astype(BF16)

    main_row = jnp.where(slot < 8, target * 8 + slot, -1)
    for b in range(4):
        chosen = flag(iota((256, ROWS), 0) == main_row - b * 256)
        out_ref[b * 256 : (b + 1) * 256, :D] = dot(chosen, unit[...]).astype(BF16)


def pack(emb, cluster, rank):
    return pl.pallas_call(
        pack_kernel,
        in_specs=[
            pl.BlockSpec(memory_space=pl.ANY),
            pl.BlockSpec(memory_space=pltpu.VMEM),
            pl.BlockSpec(memory_space=pltpu.VMEM),
        ],
        out_shape=(
            jax.ShapeDtypeStruct((MAIN, D + 256), BF16),
            jax.ShapeDtypeStruct((2, ROWS), I32),
        ),
        scratch_shapes=[
            pltpu.VMEM((ROWS, D), BF16),
            pltpu.VMEM((ROWS, D), BF16),
            pltpu.VMEM((MAIN, 128), F32),
            pltpu.VMEM((MAIN, 128), F32),
            pltpu.SemaphoreType.DMA((4,)),
        ],
        compiler_params=LIMIT,
        name="pack",
    )(emb, cluster.reshape(1, ROWS), rank.reshape(1, ROWS))


def unpack_kernel(got_ref, late_ref, meta_ref, near_ref, far_ref, bad_ref, left, right):
    left[...] = got_ref[:, D : D + 128].astype(F32)
    right[...] = got_ref[:, D + 128 :].astype(F32)
    for k in range(2):
        for piece in range(3):
            for half, ref in enumerate((left, right)):
                at = piece * 256 + half * 128
                late_ref[k * N : (k + 1) * N, at : at + 128] = ref[
                    pl.ds(2 * piece + k, N, stride=8), :
                ].astype(BF16)
    meta = left[pl.ds(6, N, stride=8), :]
    queue = right[pl.ds(6, N, stride=8), :]
    meta_ref[...] = meta

    over_near = jnp.sum(jnp.minimum(queue, float(SLOTS)), axis=0, keepdims=True) - NEAR
    over_far = (
        jnp.sum(jnp.clip(queue - SLOTS, 0.0, float(SLOTS)), axis=0, keepdims=True) - FAR
    )
    over_long = jnp.max(queue, axis=0, keepdims=True) - 2.0 * SLOTS
    bad_ref[0, 0] = (
        jnp.max(jnp.maximum(jnp.maximum(over_near, over_far), over_long)) > 0.0
    ).astype(I32)

    lane = iota((N, N), 1)
    hops = pltpu.roll(meta, N - 16, 1)
    moves = (lane < SLOTS) & (meta > 0.0)
    one = flag(moves & (hops == 1.0))
    two = flag(moves & (hops == 2.0))
    each = dot_nt(jnp.ones((8, N), BF16), jnp.concatenate([one, two], axis=0))
    first = dot(
        jnp.concatenate([each[:, :N], each[:, N:]], axis=0).astype(BF16),
        flag(iota((N, N), 0) < iota((N, N), 1)),
    )
    count_one, count_two = each[0:1, :N], each[0:1, N:]
    first_one, first_two = first[0:1], first[8:9]

    def rows_of(length, first, count, skip):
        line = iota((length, N), 0).astype(F32)
        mine = (line >= first) & (line < first + count)
        source = jnp.sum(jnp.where(mine, iota((length, N), 1).astype(F32), 0.0), 1, keepdims=True)
        place = jnp.sum(jnp.where(mine, line - first + skip, 0.0), 1, keepdims=True)
        any_row = line[:, :1] < jnp.sum(count, 1, keepdims=True)
        return flag(mine), source.astype(I32), place.astype(I32), any_row

    near = rows_of(NEAR, first_one, count_one, count_two)
    far = rows_of(FAR, first_two, count_two, 0.0)
    mine, source, slot = (jnp.concatenate([a, b], axis=0) for a, b in zip(near[:3], far[:3]))
    used = jnp.concatenate([near[3].astype(I32), far[3].astype(I32)], axis=0) > 0

    at_main = jnp.where(used & (slot < 8), source * 8 + slot, -1)
    at_late = jnp.where(used & (slot >= 8), (slot - 8) * N + source, -1)
    sent = dot(flag(iota((MOVED, MAIN), 1) == at_main), got_ref[:, :D]) + dot(
        flag(iota((MOVED, EXTRA), 1) == at_late), late_ref[...]
    )
    sent = sent.astype(BF16)
    card = dot(mine, meta.astype(BF16))
    lanes = iota((MOVED, META), 1)
    card = jnp.where((lanes & 15) == slot, card, 0.0)
    card = jnp.where(lanes == 96, source.astype(F32), card)
    card = jnp.where(lanes == 97, slot.astype(F32), card).astype(BF16)
    near_ref[:, :D] = sent[:NEAR]
    near_ref[:, D:] = card[:NEAR]
    far_ref[:, :D] = sent[NEAR:]
    far_ref[:, D:] = card[NEAR:]


def unpack(got):
    return pl.pallas_call(
        unpack_kernel,
        out_shape=(
            jax.ShapeDtypeStruct((EXTRA, D), BF16),
            jax.ShapeDtypeStruct((N, META), F32),
            jax.ShapeDtypeStruct((NEAR, D + META), BF16),
            jax.ShapeDtypeStruct((FAR, D + META), BF16),
            jax.ShapeDtypeStruct((1, 1), I32),
        ),
        out_specs=(pl.BlockSpec(memory_space=pltpu.VMEM),) * 4
        + (pl.BlockSpec(memory_space=pltpu.SMEM),),
        scratch_shapes=[pltpu.VMEM((MAIN, 128), F32), pltpu.VMEM((MAIN, 128), F32)],
        compiler_params=LIMIT,
        name="unpack",
    )(got)


RANK = ((2, 1.0), (3, 256.0), (4, 65536.0))
CLUSTER = ((0, 1.0), (1, -16.0))


def local_kernel(got_ref, late_ref, meta_ref, row_ref, best_ref, own, column):
    meta = meta_ref[...]
    spread = dot(flag((iota((MAIN, N), 0) >> 3) == iota((MAIN, N), 1)), meta.astype(BF16))
    own[:MAIN, :] = jnp.where(
        (iota((MAIN, N), 1) & 15) == (iota((MAIN, N), 0) & 7), spread, 0.0
    ).astype(BF16)
    lane = iota((N, N), 1) & 15
    for k in range(2):
        own[MAIN + k * N : MAIN + (k + 1) * N, :] = jnp.where(lane == 8 + k, meta, 0.0).astype(BF16)
    row_ref[...] = dot_nt(
        jnp.concatenate([weights(RANK, (8, N), 1), weights(CLUSTER, (8, N), 1)], axis=0), own[...]
    )
    column[...] = dot(
        own[...],
        jnp.concatenate([weights(RANK, (N, N), 0), weights(CLUSTER, (N, N), 0)], axis=1),
    )
    best_ref[...] = jnp.full((8, ALL), -1.0, F32)

    def rows_of(b):
        if b * 256 < MAIN:
            return got_ref[b * 256 : (b + 1) * 256, :D]
        return late_ref[...]

    blocks = ALL // 256
    for i in range(blocks):
        rank = column[i * 256 : (i + 1) * 256, :128]
        cluster = column[i * 256 : (i + 1) * 256, 128:]
        rank = jnp.concatenate([rank, rank], axis=1)
        cluster = jnp.concatenate([cluster, cluster], axis=1)
        for j in range(blocks):
            across = slice(j * 256, (j + 1) * 256)
            similar = dot_nt(rows_of(i), rows_of(j))
            earlier = (cluster == row_ref[8:9, across]) & (rank < row_ref[0:1, across])
            kept = jnp.where(earlier, similar, -1.0)
            best_ref[:, across] = jnp.maximum(
                best_ref[:, across], jnp.max(kept.reshape(32, 8, 256), axis=0)
            )


def local_best(got, late, meta):
    return pl.pallas_call(
        local_kernel,
        out_shape=(
            jax.ShapeDtypeStruct((16, ALL), F32),
            jax.ShapeDtypeStruct((8, ALL), F32),
        ),
        scratch_shapes=[pltpu.VMEM((ALL, N), BF16), pltpu.VMEM((ALL, 256), F32)],
        compiler_params=LIMIT,
        cost_estimate=pl.CostEstimate(
            flops=2 * ALL * ALL * D, bytes_accessed=4 * ALL * D, transcendentals=0
        ),
        name="local_best",
    )(got, late, meta)


def cross_kernel(got_ref, late_ref, row_ref, best_ref, near_ref, far_ref, out_ref, moved):
    moved[0:NEAR, :] = near_ref[...]
    moved[NEAR:, :] = far_ref[...]
    card = moved[:, D:]
    column = dot(
        card,
        jnp.concatenate(
            [
                weights(RANK, (META, 128), 0),
                weights(CLUSTER[:1], (META, 128), 0),
                weights(((96, 1.0),), (META, 128), 0, 1),
                weights(((97, 1.0),), (META, 128), 0, 1),
            ],
            axis=1,
        ),
    )
    rank, cluster = column[:, :128], column[:, 128:256]
    source, slot = column[:, 256:384].astype(I32), column[:, 384:].astype(I32)
    moved_row = dot_nt(
        jnp.concatenate([weights(RANK, (8, META), 1), weights(CLUSTER[:1], (8, META), 1)], axis=0),
        card,
    )
    rank2 = jnp.concatenate([rank, rank], axis=1)
    cluster2 = jnp.concatenate([cluster, cluster], axis=1)

    unit = moved[:, :D]
    arrived = jnp.full((MOVED, 256), -1.0, F32)
    bests = []
    for j in range(ALL // 256):
        across = slice(j * 256, (j + 1) * 256)
        rows = got_ref[across, :D] if j * 256 < MAIN else late_ref[...]
        similar = dot_nt(unit, rows)
        same = cluster2 == row_ref[8:9, across]
        earlier = rank2 < row_ref[0:1, across]
        kept = jnp.where(same & earlier, similar, -1.0)
        here = jnp.maximum(best_ref[:, across], jnp.max(kept.reshape(MOVED // 8, 8, 256), axis=0))
        bests.append(jnp.max(here, axis=0, keepdims=True))
        later = rank2 > row_ref[0:1, across]
        arrived = jnp.maximum(arrived, jnp.where(same & later, similar, -1.0))
    similar = dot_nt(unit, unit)
    later = (cluster2[:, :MOVED] == moved_row[8:9]) & (rank2[:, :MOVED] > moved_row[0:1])
    arrived = jnp.maximum(
        jnp.max(arrived, axis=1, keepdims=True),
        jnp.max(jnp.where(later, similar, -1.0), axis=1, keepdims=True),
    )

    main = jnp.concatenate(bests[: MAIN // 256], axis=1)
    main = jnp.where((iota((8, MAIN), 1) & 7) == iota((8, MAIN), 0), main, 0.0)
    of_sender = flag((iota((MAIN, N), 0) >> 3) == iota((MAIN, N), 1))
    answers = sum(dot(part, of_sender) for part in parts(main))
    late = bests[MAIN // 256]
    answers = jnp.concatenate(
        [answers, late[:, :N], late[:, N:], jnp.zeros((N - SLOTS, N), F32)], axis=0
    )
    hop = jnp.where(iota((MOVED, N), 0) < NEAR, 16, 32)
    by_lane = jnp.where((cluster > 0.0) & (iota((MOVED, N), 1) == hop + slot), arrived, 0.0)
    sender = flag((cluster > 0.0) & (iota((MOVED, N), 1) == source), F32).T.astype(BF16)
    out_ref[...] = answers.T + sum(dot(sender, part) for part in parts(by_lane))


def cross_best(got, late, row, best, near, far):
    return pl.pallas_call(
        cross_kernel,
        out_shape=jax.ShapeDtypeStruct((N, N), F32),
        scratch_shapes=[pltpu.VMEM((MOVED, D + META), BF16)],
        compiler_params=LIMIT,
        name="cross_best",
    )(got, late, row, best, near, far)


def pick_kernel(back_ref, place_ref, out_ref):
    home = place_ref[0:1, :]
    lane = place_ref[1:2, :]
    at_home = flag(iota((N, ROWS), 0) == home)
    table = sum(dot(part, at_home) for part in parts(back_ref[...].T[:48]))
    out_ref[...] = jnp.sum(
        jnp.where(iota((48, ROWS), 0) == lane, table, 0.0), axis=0, keepdims=True
    )


def pick(back, place):
    return pl.pallas_call(
        pick_kernel,
        out_shape=jax.ShapeDtypeStruct((1, ROWS), F32),
        compiler_params=LIMIT,
        name="pick",
    )(back, place)


def passed_along(array, by):
    return lax.ppermute(array, "dev", [(i, (i + by) % N) for i in range(N)])


def moved_back(array, by):
    pairs = [(device_at(i), device_at((i - by) % N)) for i in range(N)]
    return lax.ppermute(array, "dev", pairs)


def swapped(array):
    return lax.all_to_all(array, "dev", split_axis=0, concat_axis=0, tiled=True)


def paired_best(left, right):
    left_unit, left_cluster, left_rank = left
    right_unit, right_cluster, right_rank = right
    block_rows = 512
    block_count = left_unit.shape[0] // block_rows
    blocked = (
        left_unit.reshape(block_count, block_rows, D),
        left_cluster.reshape(block_count, block_rows),
        left_rank.reshape(block_count, block_rows),
    )

    def advance(carry, pieces):
        unit, cluster, rank = pieces
        similar = dot_nt(unit, right_unit)
        same = (cluster[:, None] == right_cluster[None, :]) & (right_cluster[None, :] >= 0)
        earlier = same & (right_rank[None, :] < rank[:, None])
        return carry, jnp.max(jnp.where(earlier, similar, -1.0), axis=1)

    return lax.scan(advance, 0, blocked)[1].reshape(-1)


def by_pools(emb, cluster, rank):
    capacity = 2 * ROWS // N
    pool_rows = N * capacity
    wide = emb.astype(F32)
    unit = (wide * lax.rsqrt(jnp.sum(wide * wide, axis=-1, keepdims=True) + 1e-06)).astype(BF16)
    target = (cluster % N + rank % 2) % N
    one_hot = (target[:, None] == jnp.arange(N, dtype=I32)[None, :]).astype(I32)
    slot = jnp.sum(jnp.cumsum(one_hot, axis=0) * one_hot, axis=1) - 1
    placing = target * capacity + slot
    received = (
        swapped(jnp.zeros((pool_rows, D), BF16).at[placing].set(unit)),
        swapped(jnp.full((pool_rows,), -1, I32).at[placing].set(cluster)),
        swapped(jnp.zeros((pool_rows,), I32).at[placing].set(rank)),
    )
    best = paired_best(received, received)
    for by in (1, -1):
        other = tuple(passed_along(part, by) for part in received)
        best = jnp.maximum(best, paired_best(received, other))
    return swapped(best)[placing]


def per_device(emb, cluster, rank):
    packed, place = pack(emb, cluster, rank)
    got = swapped(packed.reshape(N, 8, D + 256)).reshape(MAIN, D + 256)
    late, meta, near, far, bad = unpack(got)
    near = moved_back(near, 1)
    far = moved_back(far, 2)
    row, best = local_best(got, late, meta)
    answers = cross_best(got, late, row, best, near, far)
    back = swapped(answers.reshape(N, 1, N)).reshape(N, N)
    nearest = pick(back, place).reshape(ROWS)
    return lax.cond(
        bad[0, 0] > 0,
        by_pools,
        lambda emb, cluster, rank: nearest,
        emb,
        cluster,
        rank,
    )


def solution(mesh):
    placed = (P("dev", None), P("dev"), P("dev"))
    return jax.shard_map(
        per_device, mesh=mesh, in_specs=placed, out_specs=P("dev"), check_vma=False
    )
```

```python
import jax
import jax.numpy as jnp
from jax import lax
from jax.experimental import pallas as pl
from jax.experimental.pallas import tpu as pltpu
from jax.sharding import PartitionSpec as P

F32 = jnp.float32
BF16 = jnp.bfloat16
I32 = jnp.int32

N = 128
ROWS = 1024
D = 768
SLOTS = 10
MAIN = 8 * N
EXTRA = 2 * N
ALL = MAIN + EXTRA
NEAR = 144
FAR = 16
MOVED = NEAR + FAR
META = 128
LIMIT = pltpu.CompilerParams(vmem_limit_bytes=20 * 1024 * 1024)


def iota(shape, dim):
    return lax.broadcasted_iota(I32, shape, dim)


def flag(mask, dtype=BF16):
    return jnp.where(mask, 1.0, 0.0).astype(dtype)


def dot(a, b):
    return jnp.dot(a, b, preferred_element_type=F32)


def dot_nt(a, b):
    return lax.dot_general(a, b, (((1,), (1,)), ((), ())), preferred_element_type=F32)


def parts(a):
    high = a.astype(BF16)
    rest = a - high.astype(F32)
    middle = rest.astype(BF16)
    return high, middle, (rest - middle.astype(F32)).astype(BF16)


def weights(rows, shape, dim, size=16):
    group = iota(shape, dim) // size
    weight = jnp.zeros(shape, F32)
    for at, by in rows:
        weight = jnp.where(group == at, by, weight)
    return weight.astype(BF16)


RING_Y = 1878693120
RING_Z = 29252580


def device_at(turn):
    place = turn >> 3
    x = ((turn >> 1) & 3) ^ ((place & 1) * 3)
    y = (RING_Y >> (place * 2)) & 3
    z = (RING_Z >> (place * 2)) & 3
    return z * 32 + y * 8 + x * 2 + (turn & 1)


def pack_kernel(
    emb_ref, cluster_ref, rank_ref, out_ref, place_ref, raw, ids, left, right, arrived
):
    loads = [
        pltpu.make_async_copy(cluster_ref, ids.at[0], arrived.at[0]),
        pltpu.make_async_copy(rank_ref, ids.at[1], arrived.at[1]),
        pltpu.make_async_copy(emb_ref, raw, arrived.at[2]),
    ]
    for load in loads:
        load.start()

    loads[0].wait()
    cluster = ids[0]
    loads[1].wait()
    rank = ids[1]
    home = cluster & (N - 1)
    member = cluster // N

    which = iota((N, ROWS), 0)
    at_home = which == home
    at_home_b = flag(at_home)
    row, column = iota((N, N), 0), iota((N, N), 1)
    upper = flag(row < column)
    count = dot_nt(jnp.ones((8, ROWS), BF16), at_home_b)
    chunks = jnp.concatenate([at_home_b[:, c * 128 : (c + 1) * 128] for c in range(8)], axis=0)
    running = dot(chunks, jnp.concatenate([upper, jnp.ones((N, N), BF16)], axis=1))
    totals = [running[c * 128 : (c + 1) * 128, 128:] for c in range(8)]
    total = sum(totals[1:], totals[0])

    over = total - float(SLOTS)
    below = dot(flag(row > column), over.astype(BF16))
    along = dot((count - float(SLOTS)).astype(BF16), upper)
    round_trip = float(ROWS - SLOTS * N)
    ahead = below + jnp.max(
        jnp.where(column < row, 0.0, round_trip) - along[:1], axis=1, keepdims=True
    )
    ahead = jnp.maximum(ahead, 0.0)
    queue = along[:1] + count[:1] - float(SLOTS)
    queue = queue + jnp.max(
        jnp.where(row <= column, 0.0, round_trip) - below, axis=0, keepdims=True
    )
    queue = jnp.maximum(queue, 0.0)

    before = ahead
    turn = []
    for c in range(8):
        part = running[c * 128 : (c + 1) * 128, :128]
        turn.append(
            jnp.sum(
                jnp.where(at_home[:, c * 128 : (c + 1) * 128], part + before, 0.0),
                axis=0,
                keepdims=True,
            )
        )
        before = before + totals[c]
    offset = jnp.concatenate(turn, axis=1)
    hops = jnp.floor((offset + 0.5) * (1.0 / SLOTS))
    slot = (offset - hops * SLOTS).astype(I32)
    hops = hops.astype(I32)
    target = device_at((home + hops) & (N - 1))
    place_ref[0:1, :] = device_at(home)
    place_ref[1:2, :] = jnp.minimum(hops, 7) * 16 + slot

    loads[2].wait()

    def unit_rows(chosen):
        wide = dot(chosen, raw[...])
        return wide * lax.rsqrt(jnp.sum(wide * wide, axis=-1, keepdims=True) + 1e-06)

    def spread(value):
        return jnp.broadcast_to(value, (16, ROWS))

    value = jnp.concatenate(
        [
            spread(member + 1),
            spread(hops),
            spread(rank & 255),
            spread((rank >> 8) & 255),
            spread(rank >> 16),
            jnp.zeros((48, ROWS), I32),
        ],
        axis=0,
    )
    value = jnp.where((iota((META, ROWS), 0) & 15) == slot, value, 0)
    meta = dot_nt(flag(which == target), value.astype(F32).astype(BF16))
    left[pl.ds(6, N, stride=8), :] = meta
    right[pl.ds(6, N, stride=8), :] = jnp.broadcast_to(jnp.minimum(queue, 255.0), (N, 128))
    left[pl.ds(7, N, stride=8), :] = jnp.zeros((N, 128), F32)
    right[pl.ds(7, N, stride=8), :] = jnp.zeros((N, 128), F32)
    extra_row = jnp.where(slot >= 8, (slot - 8) * N + target, -1)
    late = unit_rows(flag(iota((EXTRA, ROWS), 0) == extra_row))
    for k in range(2):
        for piece in range(3):
            rows = late[k * N : (k + 1) * N, piece * 256 : (piece + 1) * 256]
            left[pl.ds(2 * piece + k, N, stride=8), :] = rows[:, :128]
            right[pl.ds(2 * piece + k, N, stride=8), :] = rows[:, 128:]
    out_ref[:, D : D + 128] = left[...].astype(BF16)
    out_ref[:, D + 128 :] = right[...].astype(BF16)

    main_row = jnp.where(slot < 8, target * 8 + slot, -1)
    for b in range(4):
        chosen = flag(iota((256, ROWS), 0) == main_row - b * 256)
        out_ref[b * 256 : (b + 1) * 256, :D] = unit_rows(chosen).astype(BF16)


def pack(emb, cluster, rank):
    return pl.pallas_call(
        pack_kernel,
        in_specs=[pl.BlockSpec(memory_space=pl.ANY)] * 3,
        out_shape=(
            jax.ShapeDtypeStruct((MAIN, D + 256), BF16),
            jax.ShapeDtypeStruct((2, ROWS), I32),
        ),
        scratch_shapes=[
            pltpu.VMEM((ROWS, D), BF16),
            pltpu.VMEM((2, 1, ROWS), I32),
            pltpu.VMEM((MAIN, 128), F32),
            pltpu.VMEM((MAIN, 128), F32),
            pltpu.SemaphoreType.DMA((3,)),
        ],
        compiler_params=LIMIT,
        name="pack",
    )(emb, cluster.reshape(1, ROWS), rank.reshape(1, ROWS))


def unpack_kernel(got_ref, late_ref, meta_ref, near_ref, far_ref, bad_ref, left, right):
    left[...] = got_ref[:, D : D + 128].astype(F32)
    right[...] = got_ref[:, D + 128 :].astype(F32)
    for k in range(2):
        for piece in range(3):
            for half, ref in enumerate((left, right)):
                at = piece * 256 + half * 128
                late_ref[k * N : (k + 1) * N, at : at + 128] = ref[
                    pl.ds(2 * piece + k, N, stride=8), :
                ].astype(BF16)
    meta = left[pl.ds(6, N, stride=8), :]
    queue = right[pl.ds(6, N, stride=8), :]
    meta_ref[...] = meta

    over_near = jnp.sum(jnp.minimum(queue, float(SLOTS)), axis=0, keepdims=True) - NEAR
    over_far = (
        jnp.sum(jnp.clip(queue - SLOTS, 0.0, float(SLOTS)), axis=0, keepdims=True) - FAR
    )
    over_long = jnp.max(queue, axis=0, keepdims=True) - 2.0 * SLOTS
    bad_ref[0, 0] = (
        jnp.max(jnp.maximum(jnp.maximum(over_near, over_far), over_long)) > 0.0
    ).astype(I32)

    lane = iota((N, N), 1)
    hops = pltpu.roll(meta, N - 16, 1)
    moves = (lane < SLOTS) & (meta > 0.0)
    one = flag(moves & (hops == 1.0))
    two = flag(moves & (hops == 2.0))
    each = dot_nt(jnp.ones((8, N), BF16), jnp.concatenate([one, two], axis=0))
    first = dot(
        jnp.concatenate([each[:, :N], each[:, N:]], axis=0).astype(BF16),
        flag(iota((N, N), 0) < iota((N, N), 1)),
    )
    count_one, count_two = each[0:1, :N], each[0:1, N:]
    first_one, first_two = first[0:1], first[8:9]

    def rows_of(length, first, count, skip):
        line = iota((length, N), 0).astype(F32)
        mine = (line >= first) & (line < first + count)
        source = jnp.sum(jnp.where(mine, iota((length, N), 1).astype(F32), 0.0), 1, keepdims=True)
        place = jnp.sum(jnp.where(mine, line - first + skip, 0.0), 1, keepdims=True)
        any_row = line[:, :1] < jnp.sum(count, 1, keepdims=True)
        return flag(mine), source.astype(I32), place.astype(I32), any_row

    near = rows_of(NEAR, first_one, count_one, count_two)
    far = rows_of(FAR, first_two, count_two, 0.0)
    mine, source, slot = (jnp.concatenate([a, b], axis=0) for a, b in zip(near[:3], far[:3]))
    used = jnp.concatenate([near[3].astype(I32), far[3].astype(I32)], axis=0) > 0

    at_main = jnp.where(used & (slot < 8), source * 8 + slot, -1)
    at_late = jnp.where(used & (slot >= 8), (slot - 8) * N + source, -1)
    sent = dot(flag(iota((MOVED, MAIN), 1) == at_main), got_ref[:, :D]) + dot(
        flag(iota((MOVED, EXTRA), 1) == at_late), late_ref[...]
    )
    sent = sent.astype(BF16)
    card = dot(mine, meta.astype(BF16))
    lanes = iota((MOVED, META), 1)
    card = jnp.where((lanes & 15) == slot, card, 0.0)
    card = jnp.where(lanes == 96, source.astype(F32), card)
    card = jnp.where(lanes == 97, slot.astype(F32), card).astype(BF16)
    near_ref[:, :D] = sent[:NEAR]
    near_ref[:, D:] = card[:NEAR]
    far_ref[:, :D] = sent[NEAR:]
    far_ref[:, D:] = card[NEAR:]


def unpack(got):
    return pl.pallas_call(
        unpack_kernel,
        out_shape=(
            jax.ShapeDtypeStruct((EXTRA, D), BF16),
            jax.ShapeDtypeStruct((N, META), F32),
            jax.ShapeDtypeStruct((NEAR, D + META), BF16),
            jax.ShapeDtypeStruct((FAR, D + META), BF16),
            jax.ShapeDtypeStruct((1, 1), I32),
        ),
        out_specs=(pl.BlockSpec(memory_space=pltpu.VMEM),) * 4
        + (pl.BlockSpec(memory_space=pltpu.SMEM),),
        scratch_shapes=[pltpu.VMEM((MAIN, 128), F32), pltpu.VMEM((MAIN, 128), F32)],
        compiler_params=LIMIT,
        name="unpack",
    )(got)


RANK = ((2, 1.0), (3, 256.0), (4, 65536.0))
CLUSTER = ((0, 1.0), (1, -16.0))


def local_kernel(got_ref, late_ref, meta_ref, row_ref, best_ref, own, column):
    meta = meta_ref[...]
    spread = dot(flag((iota((MAIN, N), 0) >> 3) == iota((MAIN, N), 1)), meta.astype(BF16))
    own[:MAIN, :] = jnp.where(
        (iota((MAIN, N), 1) & 15) == (iota((MAIN, N), 0) & 7), spread, 0.0
    ).astype(BF16)
    lane = iota((N, N), 1) & 15
    for k in range(2):
        own[MAIN + k * N : MAIN + (k + 1) * N, :] = jnp.where(lane == 8 + k, meta, 0.0).astype(BF16)
    row_ref[...] = dot_nt(
        jnp.concatenate([weights(RANK, (8, N), 1), weights(CLUSTER, (8, N), 1)], axis=0), own[...]
    )
    column[...] = dot(
        own[...],
        jnp.concatenate([weights(RANK, (N, N), 0), weights(CLUSTER, (N, N), 0)], axis=1),
    )
    best_ref[...] = jnp.full((8, ALL), -1.0, F32)

    def rows_of(b):
        if b * 256 < MAIN:
            return got_ref[b * 256 : (b + 1) * 256, :D]
        return late_ref[...]

    blocks = ALL // 256
    for i in range(blocks):
        rank = column[i * 256 : (i + 1) * 256, :128]
        cluster = column[i * 256 : (i + 1) * 256, 128:]
        rank = jnp.concatenate([rank, rank], axis=1)
        cluster = jnp.concatenate([cluster, cluster], axis=1)
        for j in range(blocks):
            across = slice(j * 256, (j + 1) * 256)
            similar = dot_nt(rows_of(i), rows_of(j))
            earlier = (cluster == row_ref[8:9, across]) & (rank < row_ref[0:1, across])
            kept = jnp.where(earlier, similar, -1.0)
            best_ref[:, across] = jnp.maximum(
                best_ref[:, across], jnp.max(kept.reshape(32, 8, 256), axis=0)
            )


def local_best(got, late, meta):
    return pl.pallas_call(
        local_kernel,
        out_shape=(
            jax.ShapeDtypeStruct((16, ALL), F32),
            jax.ShapeDtypeStruct((8, ALL), F32),
        ),
        scratch_shapes=[pltpu.VMEM((ALL, N), BF16), pltpu.VMEM((ALL, 256), F32)],
        compiler_params=LIMIT,
        cost_estimate=pl.CostEstimate(
            flops=2 * ALL * ALL * D, bytes_accessed=4 * ALL * D, transcendentals=0
        ),
        name="local_best",
    )(got, late, meta)


def cross_kernel(got_ref, late_ref, row_ref, best_ref, near_ref, far_ref, out_ref, moved):
    moved[0:NEAR, :] = near_ref[...]
    moved[NEAR:, :] = far_ref[...]
    card = moved[:, D:]
    column = dot(
        card,
        jnp.concatenate(
            [
                weights(RANK, (META, 128), 0),
                weights(CLUSTER[:1], (META, 128), 0),
                weights(((96, 1.0),), (META, 128), 0, 1),
                weights(((97, 1.0),), (META, 128), 0, 1),
            ],
            axis=1,
        ),
    )
    rank, cluster = column[:, :128], column[:, 128:256]
    source, slot = column[:, 256:384].astype(I32), column[:, 384:].astype(I32)
    moved_row = dot_nt(
        jnp.concatenate([weights(RANK, (8, META), 1), weights(CLUSTER[:1], (8, META), 1)], axis=0),
        card,
    )
    rank2 = jnp.concatenate([rank, rank], axis=1)
    cluster2 = jnp.concatenate([cluster, cluster], axis=1)

    unit = moved[:, :D]
    arrived = jnp.full((MOVED, 256), -1.0, F32)
    bests = []
    for j in range(ALL // 256):
        across = slice(j * 256, (j + 1) * 256)
        rows = got_ref[across, :D] if j * 256 < MAIN else late_ref[...]
        similar = dot_nt(unit, rows)
        same = cluster2 == row_ref[8:9, across]
        earlier = rank2 < row_ref[0:1, across]
        kept = jnp.where(same & earlier, similar, -1.0)
        here = jnp.maximum(best_ref[:, across], jnp.max(kept.reshape(MOVED // 8, 8, 256), axis=0))
        bests.append(jnp.max(here, axis=0, keepdims=True))
        later = rank2 > row_ref[0:1, across]
        arrived = jnp.maximum(arrived, jnp.where(same & later, similar, -1.0))
    similar = dot_nt(unit, unit)
    later = (cluster2[:, :MOVED] == moved_row[8:9]) & (rank2[:, :MOVED] > moved_row[0:1])
    arrived = jnp.maximum(
        jnp.max(arrived, axis=1, keepdims=True),
        jnp.max(jnp.where(later, similar, -1.0), axis=1, keepdims=True),
    )

    main = jnp.concatenate(bests[: MAIN // 256], axis=1)
    main = jnp.where((iota((8, MAIN), 1) & 7) == iota((8, MAIN), 0), main, 0.0)
    of_sender = flag((iota((MAIN, N), 0) >> 3) == iota((MAIN, N), 1))
    answers = sum(dot(part, of_sender) for part in parts(main))
    late = bests[MAIN // 256]
    answers = jnp.concatenate(
        [answers, late[:, :N], late[:, N:], jnp.zeros((N - SLOTS, N), F32)], axis=0
    )
    hop = jnp.where(iota((MOVED, N), 0) < NEAR, 16, 32)
    by_lane = jnp.where((cluster > 0.0) & (iota((MOVED, N), 1) == hop + slot), arrived, 0.0)
    sender = flag((cluster > 0.0) & (iota((MOVED, N), 1) == source), F32).T.astype(BF16)
    out_ref[...] = answers.T + sum(dot(sender, part) for part in parts(by_lane))


def cross_best(got, late, row, best, near, far):
    return pl.pallas_call(
        cross_kernel,
        out_shape=jax.ShapeDtypeStruct((N, N), F32),
        scratch_shapes=[pltpu.VMEM((MOVED, D + META), BF16)],
        compiler_params=LIMIT,
        name="cross_best",
    )(got, late, row, best, near, far)


def pick_kernel(back_ref, place_ref, out_ref):
    home = place_ref[0:1, :]
    lane = place_ref[1:2, :]
    at_home = flag(iota((N, ROWS), 0) == home)
    table = sum(dot(part, at_home) for part in parts(back_ref[...].T[:48]))
    out_ref[...] = jnp.sum(
        jnp.where(iota((48, ROWS), 0) == lane, table, 0.0), axis=0, keepdims=True
    )


def pick(back, place):
    return pl.pallas_call(
        pick_kernel,
        out_shape=jax.ShapeDtypeStruct((1, ROWS), F32),
        compiler_params=LIMIT,
        name="pick",
    )(back, place)


def passed_along(array, by):
    return lax.ppermute(array, "dev", [(i, (i + by) % N) for i in range(N)])


def moved_back(array, by):
    pairs = [(device_at(i), device_at((i - by) % N)) for i in range(N)]
    return lax.ppermute(array, "dev", pairs)


def swapped(array):
    return lax.all_to_all(array, "dev", split_axis=0, concat_axis=0, tiled=True)


def paired_best(left, right):
    left_unit, left_cluster, left_rank = left
    right_unit, right_cluster, right_rank = right
    block_rows = 512
    block_count = left_unit.shape[0] // block_rows
    blocked = (
        left_unit.reshape(block_count, block_rows, D),
        left_cluster.reshape(block_count, block_rows),
        left_rank.reshape(block_count, block_rows),
    )

    def advance(carry, pieces):
        unit, cluster, rank = pieces
        similar = dot_nt(unit, right_unit)
        same = (cluster[:, None] == right_cluster[None, :]) & (right_cluster[None, :] >= 0)
        earlier = same & (right_rank[None, :] < rank[:, None])
        return carry, jnp.max(jnp.where(earlier, similar, -1.0), axis=1)

    return lax.scan(advance, 0, blocked)[1].reshape(-1)


def by_pools(emb, cluster, rank):
    capacity = 2 * ROWS // N
    pool_rows = N * capacity
    wide = emb.astype(F32)
    unit = (wide * lax.rsqrt(jnp.sum(wide * wide, axis=-1, keepdims=True) + 1e-06)).astype(BF16)
    target = (cluster % N + rank % 2) % N
    one_hot = (target[:, None] == jnp.arange(N, dtype=I32)[None, :]).astype(I32)
    slot = jnp.sum(jnp.cumsum(one_hot, axis=0) * one_hot, axis=1) - 1
    placing = target * capacity + slot
    received = (
        swapped(jnp.zeros((pool_rows, D), BF16).at[placing].set(unit)),
        swapped(jnp.full((pool_rows,), -1, I32).at[placing].set(cluster)),
        swapped(jnp.zeros((pool_rows,), I32).at[placing].set(rank)),
    )
    best = paired_best(received, received)
    for by in (1, -1):
        other = tuple(passed_along(part, by) for part in received)
        best = jnp.maximum(best, paired_best(received, other))
    return swapped(best)[placing]


def per_device(emb, cluster, rank):
    packed, place = pack(emb, cluster, rank)
    got = swapped(packed.reshape(N, 8, D + 256)).reshape(MAIN, D + 256)
    late, meta, near, far, bad = unpack(got)
    near = moved_back(near, 1)
    far = moved_back(far, 2)
    row, best = local_best(got, late, meta)
    answers = cross_best(got, late, row, best, near, far)
    back = swapped(answers.reshape(N, 1, N)).reshape(N, N)
    nearest = pick(back, place).reshape(ROWS)
    return lax.cond(
        bad[0, 0] > 0,
        by_pools,
        lambda emb, cluster, rank: nearest,
        emb,
        cluster,
        rank,
    )


def solution(mesh):
    placed = (P("dev", None), P("dev"), P("dev"))
    return jax.shard_map(
        per_device, mesh=mesh, in_specs=placed, out_specs=P("dev"), check_vma=False
    )
```

```python
import jax
import jax.numpy as jnp
from jax import lax
from jax.experimental import pallas as pl
from jax.experimental.pallas import tpu as pltpu
from jax.sharding import PartitionSpec as P

F32 = jnp.float32
BF16 = jnp.bfloat16
I32 = jnp.int32

N = 128
ROWS = 1024
D = 768
SLOTS = 10
MAIN = 8 * N
EXTRA = 2 * N
ALL = MAIN + EXTRA
NEAR = 144
FAR = 16
MOVED = NEAR + FAR
META = 128
LIMIT = pltpu.CompilerParams(vmem_limit_bytes=20 * 1024 * 1024)


def iota(shape, dim):
    return lax.broadcasted_iota(I32, shape, dim)


def flag(mask, dtype=BF16):
    return jnp.where(mask, 1.0, 0.0).astype(dtype)


def dot(a, b):
    return jnp.dot(a, b, preferred_element_type=F32)


def dot_nt(a, b):
    return lax.dot_general(a, b, (((1,), (1,)), ((), ())), preferred_element_type=F32)


def parts(a):
    high = a.astype(BF16)
    rest = a - high.astype(F32)
    middle = rest.astype(BF16)
    return high, middle, (rest - middle.astype(F32)).astype(BF16)


def weights(rows, shape, dim, size=16):
    group = iota(shape, dim) // size
    weight = jnp.zeros(shape, F32)
    for at, by in rows:
        weight = jnp.where(group == at, by, weight)
    return weight.astype(BF16)


RING_Y = 1878693120
RING_Z = 29252580


def device_at(turn):
    place = turn >> 3
    x = ((turn >> 1) & 3) ^ ((place & 1) * 3)
    y = (RING_Y >> (place * 2)) & 3
    z = (RING_Z >> (place * 2)) & 3
    return z * 32 + y * 8 + x * 2 + (turn & 1)


def pack_kernel(
    emb_ref, cluster_ref, rank_ref, out_ref, place_ref, raw, ids, left, right, arrived
):
    loads = [
        pltpu.make_async_copy(cluster_ref, ids.at[0], arrived.at[0]),
        pltpu.make_async_copy(rank_ref, ids.at[1], arrived.at[1]),
        pltpu.make_async_copy(emb_ref, raw, arrived.at[2]),
    ]
    for load in loads:
        load.start()

    loads[0].wait()
    cluster = ids[0]
    loads[1].wait()
    rank = ids[1]
    home = cluster & (N - 1)
    member = cluster // N

    which = iota((N, ROWS), 0)
    at_home = which == home
    at_home_b = flag(at_home)
    row, column = iota((N, N), 0), iota((N, N), 1)
    upper = flag(row < column)
    count = dot_nt(jnp.ones((8, ROWS), BF16), at_home_b)
    chunks = jnp.concatenate([at_home_b[:, c * 128 : (c + 1) * 128] for c in range(8)], axis=0)
    running = dot(chunks, jnp.concatenate([upper, jnp.ones((N, N), BF16)], axis=1))
    totals = [running[c * 128 : (c + 1) * 128, 128:] for c in range(8)]
    total = sum(totals[1:], totals[0])

    over = total - float(SLOTS)
    below = dot(flag(row > column), over.astype(BF16))
    along = dot((count - float(SLOTS)).astype(BF16), upper)
    round_trip = float(ROWS - SLOTS * N)
    ahead = below + jnp.max(
        jnp.where(column < row, 0.0, round_trip) - along[:1], axis=1, keepdims=True
    )
    ahead = jnp.maximum(ahead, 0.0)
    queue = along[:1] + count[:1] - float(SLOTS)
    queue = queue + jnp.max(
        jnp.where(row <= column, 0.0, round_trip) - below, axis=0, keepdims=True
    )
    queue = jnp.maximum(queue, 0.0)

    before = ahead
    turn = []
    for c in range(8):
        part = running[c * 128 : (c + 1) * 128, :128]
        turn.append(
            jnp.sum(
                jnp.where(at_home[:, c * 128 : (c + 1) * 128], part + before, 0.0),
                axis=0,
                keepdims=True,
            )
        )
        before = before + totals[c]
    offset = jnp.concatenate(turn, axis=1)
    hops = jnp.floor((offset + 0.5) * (1.0 / SLOTS))
    slot = (offset - hops * SLOTS).astype(I32)
    hops = hops.astype(I32)
    target = device_at((home + hops) & (N - 1))
    place_ref[0:1, :] = device_at(home)
    place_ref[1:2, :] = jnp.minimum(hops, 7) * 16 + slot

    loads[2].wait()

    def unit_rows(chosen):
        wide = dot(chosen, raw[...])
        return wide * lax.rsqrt(jnp.sum(wide * wide, axis=-1, keepdims=True) + 1e-06)

    def spread(value):
        return jnp.broadcast_to(value, (16, ROWS))

    value = jnp.concatenate(
        [
            spread(member + 1),
            spread(hops),
            spread(rank & 255),
            spread((rank >> 8) & 255),
            spread(rank >> 16),
            jnp.zeros((48, ROWS), I32),
        ],
        axis=0,
    )
    value = jnp.where((iota((META, ROWS), 0) & 15) == slot, value, 0)
    meta = dot_nt(flag(which == target), value.astype(F32).astype(BF16))
    left[pl.ds(6, N, stride=8), :] = meta
    right[pl.ds(6, N, stride=8), :] = jnp.broadcast_to(jnp.minimum(queue, 255.0), (N, 128))
    left[pl.ds(7, N, stride=8), :] = jnp.zeros((N, 128), F32)
    right[pl.ds(7, N, stride=8), :] = jnp.zeros((N, 128), F32)
    extra_row = jnp.where(slot >= 8, (slot - 8) * N + target, -1)
    late = unit_rows(flag(iota((EXTRA, ROWS), 0) == extra_row))
    for k in range(2):
        for piece in range(3):
            rows = late[k * N : (k + 1) * N, piece * 256 : (piece + 1) * 256]
            left[pl.ds(2 * piece + k, N, stride=8), :] = rows[:, :128]
            right[pl.ds(2 * piece + k, N, stride=8), :] = rows[:, 128:]
    out_ref[:, D : D + 128] = left[...].astype(BF16)
    out_ref[:, D + 128 :] = right[...].astype(BF16)

    main_row = jnp.where(slot < 8, target * 8 + slot, -1)
    for b in range(4):
        chosen = flag(iota((256, ROWS), 0) == main_row - b * 256)
        out_ref[b * 256 : (b + 1) * 256, :D] = unit_rows(chosen).astype(BF16)


def pack(emb, cluster, rank):
    return pl.pallas_call(
        pack_kernel,
        in_specs=[pl.BlockSpec(memory_space=pl.ANY)] * 3,
        out_shape=(
            jax.ShapeDtypeStruct((MAIN, D + 256), BF16),
            jax.ShapeDtypeStruct((2, ROWS), I32),
        ),
        scratch_shapes=[
            pltpu.VMEM((ROWS, D), BF16),
            pltpu.VMEM((2, 1, ROWS), I32),
            pltpu.VMEM((MAIN, 128), F32),
            pltpu.VMEM((MAIN, 128), F32),
            pltpu.SemaphoreType.DMA((3,)),
        ],
        compiler_params=LIMIT,
        name="pack",
    )(emb, cluster.reshape(1, ROWS), rank.reshape(1, ROWS))


def unpack_kernel(got_ref, late_ref, meta_ref, near_ref, far_ref, bad_ref, left, right):
    left[...] = got_ref[:, D : D + 128].astype(F32)
    right[...] = got_ref[:, D + 128 :].astype(F32)
    for k in range(2):
        for piece in range(3):
            for half, ref in enumerate((left, right)):
                at = piece * 256 + half * 128
                late_ref[k * N : (k + 1) * N, at : at + 128] = ref[
                    pl.ds(2 * piece + k, N, stride=8), :
                ].astype(BF16)
    meta = left[pl.ds(6, N, stride=8), :]
    queue = right[pl.ds(6, N, stride=8), :]
    meta_ref[...] = meta

    over_near = jnp.sum(jnp.minimum(queue, float(SLOTS)), axis=0, keepdims=True) - NEAR
    over_far = (
        jnp.sum(jnp.clip(queue - SLOTS, 0.0, float(SLOTS)), axis=0, keepdims=True) - FAR
    )
    over_long = jnp.max(queue, axis=0, keepdims=True) - 2.0 * SLOTS
    bad_ref[0, 0] = (
        jnp.max(jnp.maximum(jnp.maximum(over_near, over_far), over_long)) > 0.0
    ).astype(I32)

    lane = iota((N, N), 1)
    hops = pltpu.roll(meta, N - 16, 1)
    moves = (lane < SLOTS) & (meta > 0.0)
    one = flag(moves & (hops == 1.0))
    two = flag(moves & (hops == 2.0))
    each = dot_nt(jnp.ones((8, N), BF16), jnp.concatenate([one, two], axis=0))
    first = dot(
        jnp.concatenate([each[:, :N], each[:, N:]], axis=0).astype(BF16),
        flag(iota((N, N), 0) < iota((N, N), 1)),
    )
    count_one, count_two = each[0:1, :N], each[0:1, N:]
    first_one, first_two = first[0:1], first[8:9]

    def rows_of(length, first, count, skip):
        line = iota((length, N), 0).astype(F32)
        mine = (line >= first) & (line < first + count)
        source = jnp.sum(jnp.where(mine, iota((length, N), 1).astype(F32), 0.0), 1, keepdims=True)
        place = jnp.sum(jnp.where(mine, line - first + skip, 0.0), 1, keepdims=True)
        any_row = line[:, :1] < jnp.sum(count, 1, keepdims=True)
        return flag(mine), source.astype(I32), place.astype(I32), any_row

    near = rows_of(NEAR, first_one, count_one, count_two)
    far = rows_of(FAR, first_two, count_two, 0.0)
    mine, source, slot = (jnp.concatenate([a, b], axis=0) for a, b in zip(near[:3], far[:3]))
    used = jnp.concatenate([near[3].astype(I32), far[3].astype(I32)], axis=0) > 0

    at_main = jnp.where(used & (slot < 8), source * 8 + slot, -1)
    at_late = jnp.where(used & (slot >= 8), (slot - 8) * N + source, -1)
    sent = dot(flag(iota((MOVED, MAIN), 1) == at_main), got_ref[:, :D]) + dot(
        flag(iota((MOVED, EXTRA), 1) == at_late), late_ref[...]
    )
    sent = sent.astype(BF16)
    card = dot(mine, meta.astype(BF16))
    lanes = iota((MOVED, META), 1)
    card = jnp.where((lanes & 15) == slot, card, 0.0)
    card = jnp.where(lanes == 96, source.astype(F32), card)
    card = jnp.where(lanes == 97, slot.astype(F32), card).astype(BF16)
    near_ref[:, :D] = sent[:NEAR]
    near_ref[:, D:] = card[:NEAR]
    far_ref[:, :D] = sent[NEAR:]
    far_ref[:, D:] = card[NEAR:]


def unpack(got):
    return pl.pallas_call(
        unpack_kernel,
        out_shape=(
            jax.ShapeDtypeStruct((EXTRA, D), BF16),
            jax.ShapeDtypeStruct((N, META), F32),
            jax.ShapeDtypeStruct((NEAR, D + META), BF16),
            jax.ShapeDtypeStruct((FAR, D + META), BF16),
            jax.ShapeDtypeStruct((1, 1), I32),
        ),
        out_specs=(pl.BlockSpec(memory_space=pltpu.VMEM),) * 4
        + (pl.BlockSpec(memory_space=pltpu.SMEM),),
        scratch_shapes=[pltpu.VMEM((MAIN, 128), F32), pltpu.VMEM((MAIN, 128), F32)],
        compiler_params=LIMIT,
        name="unpack",
    )(got)


RANK = ((2, 1.0), (3, 256.0), (4, 65536.0))
CLUSTER = ((0, 1.0), (1, -16.0))


def local_kernel(got_ref, late_ref, meta_ref, row_ref, best_ref, own, column):
    meta = meta_ref[...]
    spread = dot(flag((iota((MAIN, N), 0) >> 3) == iota((MAIN, N), 1)), meta.astype(BF16))
    own[:MAIN, :] = jnp.where(
        (iota((MAIN, N), 1) & 15) == (iota((MAIN, N), 0) & 7), spread, 0.0
    ).astype(BF16)
    lane = iota((N, N), 1) & 15
    for k in range(2):
        own[MAIN + k * N : MAIN + (k + 1) * N, :] = jnp.where(lane == 8 + k, meta, 0.0).astype(BF16)
    row_ref[...] = dot_nt(
        jnp.concatenate([weights(RANK, (8, N), 1), weights(CLUSTER, (8, N), 1)], axis=0), own[...]
    )
    column[...] = dot(
        own[...],
        jnp.concatenate([weights(RANK, (N, N), 0), weights(CLUSTER, (N, N), 0)], axis=1),
    )
    best_ref[...] = jnp.full((8, ALL), -1.0, F32)

    def rows_of(b):
        if b * 256 < MAIN:
            return got_ref[b * 256 : (b + 1) * 256, :D]
        return late_ref[...]

    blocks = ALL // 256
    for i in range(blocks):
        rank = column[i * 256 : (i + 1) * 256, :128]
        cluster = column[i * 256 : (i + 1) * 256, 128:]
        rank = jnp.concatenate([rank, rank], axis=1)
        cluster = jnp.concatenate([cluster, cluster], axis=1)
        for j in range(blocks):
            across = slice(j * 256, (j + 1) * 256)
            similar = dot_nt(rows_of(i), rows_of(j))
            earlier = (cluster == row_ref[8:9, across]) & (rank < row_ref[0:1, across])
            kept = jnp.where(earlier, similar, -1.0)
            best_ref[:, across] = jnp.maximum(
                best_ref[:, across], jnp.max(kept.reshape(32, 8, 256), axis=0)
            )


def local_best(got, late, meta):
    return pl.pallas_call(
        local_kernel,
        out_shape=(
            jax.ShapeDtypeStruct((16, ALL), F32),
            jax.ShapeDtypeStruct((8, ALL), F32),
        ),
        scratch_shapes=[pltpu.VMEM((ALL, N), BF16), pltpu.VMEM((ALL, 256), F32)],
        compiler_params=LIMIT,
        cost_estimate=pl.CostEstimate(
            flops=2 * ALL * ALL * D, bytes_accessed=4 * ALL * D, transcendentals=0
        ),
        name="local_best",
    )(got, late, meta)


def cross_kernel(got_ref, late_ref, row_ref, best_ref, near_ref, far_ref, out_ref, moved):
    moved[0:NEAR, :] = near_ref[...]
    moved[NEAR:, :] = far_ref[...]
    card = moved[:, D:]
    column = dot(
        card,
        jnp.concatenate(
            [
                weights(RANK, (META, 128), 0),
                weights(CLUSTER[:1], (META, 128), 0),
                weights(((96, 1.0),), (META, 128), 0, 1),
                weights(((97, 1.0),), (META, 128), 0, 1),
            ],
            axis=1,
        ),
    )
    rank, cluster = column[:, :128], column[:, 128:256]
    source, slot = column[:, 256:384].astype(I32), column[:, 384:].astype(I32)
    moved_row = dot_nt(
        jnp.concatenate([weights(RANK, (8, META), 1), weights(CLUSTER[:1], (8, META), 1)], axis=0),
        card,
    )
    rank2 = jnp.concatenate([rank, rank], axis=1)
    cluster2 = jnp.concatenate([cluster, cluster], axis=1)

    unit = moved[:, :D]
    arrived = jnp.full((MOVED, 256), -1.0, F32)
    bests = []
    for j in range(ALL // 256):
        across = slice(j * 256, (j + 1) * 256)
        rows = got_ref[across, :D] if j * 256 < MAIN else late_ref[...]
        similar = dot_nt(unit, rows)
        same = cluster2 == row_ref[8:9, across]
        earlier = rank2 < row_ref[0:1, across]
        kept = jnp.where(same & earlier, similar, -1.0)
        here = jnp.maximum(best_ref[:, across], jnp.max(kept.reshape(MOVED // 8, 8, 256), axis=0))
        bests.append(jnp.max(here, axis=0, keepdims=True))
        later = rank2 > row_ref[0:1, across]
        arrived = jnp.maximum(arrived, jnp.where(same & later, similar, -1.0))
    similar = dot_nt(unit, unit)
    later = (cluster2[:, :MOVED] == moved_row[8:9]) & (rank2[:, :MOVED] > moved_row[0:1])
    arrived = jnp.maximum(
        jnp.max(arrived, axis=1, keepdims=True),
        jnp.max(jnp.where(later, similar, -1.0), axis=1, keepdims=True),
    )

    main = jnp.concatenate(bests[: MAIN // 256], axis=1)
    main = jnp.where((iota((8, MAIN), 1) & 7) == iota((8, MAIN), 0), main, 0.0)
    of_sender = flag((iota((MAIN, N), 0) >> 3) == iota((MAIN, N), 1))
    answers = sum(dot(part, of_sender) for part in parts(main))
    late = bests[MAIN // 256]
    answers = jnp.concatenate(
        [answers, late[:, :N], late[:, N:], jnp.zeros((N - SLOTS, N), F32)], axis=0
    )
    hop = jnp.where(iota((MOVED, N), 0) < NEAR, 16, 32)
    by_lane = jnp.where((cluster > 0.0) & (iota((MOVED, N), 1) == hop + slot), arrived, 0.0)
    sender = flag((cluster > 0.0) & (iota((MOVED, N), 1) == source), F32).T.astype(BF16)
    out_ref[...] = answers.T + sum(dot(sender, part) for part in parts(by_lane))


def cross_best(got, late, row, best, near, far):
    return pl.pallas_call(
        cross_kernel,
        out_shape=jax.ShapeDtypeStruct((N, N), F32),
        scratch_shapes=[pltpu.VMEM((MOVED, D + META), BF16)],
        compiler_params=LIMIT,
        name="cross_best",
    )(got, late, row, best, near, far)


def pick_kernel(back_ref, place_ref, out_ref):
    home = place_ref[0:1, :]
    lane = place_ref[1:2, :]
    at_home = flag(iota((N, ROWS), 0) == home)
    table = sum(dot(part, at_home) for part in parts(back_ref[...].T[:48]))
    out_ref[...] = jnp.sum(
        jnp.where(iota((48, ROWS), 0) == lane, table, 0.0), axis=0, keepdims=True
    )


def pick(back, place):
    return pl.pallas_call(
        pick_kernel,
        out_shape=jax.ShapeDtypeStruct((1, ROWS), F32),
        compiler_params=LIMIT,
        name="pick",
    )(back, place)


def passed_along(array, by):
    return lax.ppermute(array, "dev", [(i, (i + by) % N) for i in range(N)])


def moved_back(array, by):
    pairs = [(device_at(i), device_at((i - by) % N)) for i in range(N)]
    return lax.ppermute(array, "dev", pairs)


def swapped(array):
    return lax.all_to_all(array, "dev", split_axis=0, concat_axis=0, tiled=True)


def paired_best(left, right):
    left_unit, left_cluster, left_rank = left
    right_unit, right_cluster, right_rank = right
    block_rows = 512
    block_count = left_unit.shape[0] // block_rows
    blocked = (
        left_unit.reshape(block_count, block_rows, D),
        left_cluster.reshape(block_count, block_rows),
        left_rank.reshape(block_count, block_rows),
    )

    def advance(carry, pieces):
        unit, cluster, rank = pieces
        similar = dot_nt(unit, right_unit)
        same = (cluster[:, None] == right_cluster[None, :]) & (right_cluster[None, :] >= 0)
        earlier = same & (right_rank[None, :] < rank[:, None])
        return carry, jnp.max(jnp.where(earlier, similar, -1.0), axis=1)

    return lax.scan(advance, 0, blocked)[1].reshape(-1)


def by_pools(emb, cluster, rank):
    capacity = 2 * ROWS // N
    pool_rows = N * capacity
    wide = emb.astype(F32)
    unit = (wide * lax.rsqrt(jnp.sum(wide * wide, axis=-1, keepdims=True) + 1e-06)).astype(BF16)
    target = (cluster % N + rank % 2) % N
    one_hot = (target[:, None] == jnp.arange(N, dtype=I32)[None, :]).astype(I32)
    slot = jnp.sum(jnp.cumsum(one_hot, axis=0) * one_hot, axis=1) - 1
    placing = target * capacity + slot
    received = (
        swapped(jnp.zeros((pool_rows, D), BF16).at[placing].set(unit)),
        swapped(jnp.full((pool_rows,), -1, I32).at[placing].set(cluster)),
        swapped(jnp.zeros((pool_rows,), I32).at[placing].set(rank)),
    )
    best = paired_best(received, received)
    for by in (1, -1):
        other = tuple(passed_along(part, by) for part in received)
        best = jnp.maximum(best, paired_best(received, other))
    return swapped(best)[placing]


def per_device(emb, cluster, rank):
    packed, place = pack(emb, cluster, rank)
    got = swapped(packed.reshape(N, 8, D + 256)).reshape(MAIN, D + 256)
    late, meta, near, far, bad = unpack(got)
    near = moved_back(near, 1)
    far = moved_back(far, 2)
    row, best = local_best(got, late, meta)
    row, bad = lax.optimization_barrier((row, bad))
    slow = bad[0, 0] > 0
    row, slow = lax.optimization_barrier((row, slow))
    answers = cross_best(got, late, row, best, near, far)
    back = swapped(answers.reshape(N, 1, N)).reshape(N, N)
    back, slow, emb, cluster, rank = lax.optimization_barrier((back, slow, emb, cluster, rank))
    nearest = pick(back, place).reshape(ROWS)
    return lax.cond(
        slow,
        by_pools,
        lambda emb, cluster, rank: nearest,
        emb,
        cluster,
        rank,
    )


def solution(mesh):
    placed = (P("dev", None), P("dev"), P("dev"))
    return jax.shard_map(
        per_device, mesh=mesh, in_specs=placed, out_specs=P("dev"), check_vma=False
    )
```

```python
import jax
import jax.numpy as jnp
from jax import lax
from jax.experimental import pallas as pl
from jax.experimental.pallas import tpu as pltpu
from jax.sharding import PartitionSpec as P

F32 = jnp.float32
BF16 = jnp.bfloat16
I32 = jnp.int32

N = 128
ROWS = 1024
D = 768
SLOTS = 10
MAIN = 8 * N
EXTRA = 2 * N
ALL = MAIN + EXTRA
NEAR = 144
FAR = 16
MOVED = NEAR + FAR
META = 128
LIMIT = pltpu.CompilerParams(vmem_limit_bytes=20 * 1024 * 1024)


def iota(shape, dim):
    return lax.broadcasted_iota(I32, shape, dim)


def flag(mask, dtype=BF16):
    return jnp.where(mask, 1.0, 0.0).astype(dtype)


def dot(a, b):
    return jnp.dot(a, b, preferred_element_type=F32)


def dot_nt(a, b):
    return lax.dot_general(a, b, (((1,), (1,)), ((), ())), preferred_element_type=F32)


def parts(a):
    high = a.astype(BF16)
    rest = a - high.astype(F32)
    middle = rest.astype(BF16)
    return high, middle, (rest - middle.astype(F32)).astype(BF16)


def weights(rows, shape, dim, size=16):
    group = iota(shape, dim) // size
    weight = jnp.zeros(shape, F32)
    for at, by in rows:
        weight = jnp.where(group == at, by, weight)
    return weight.astype(BF16)


RING_Y = 1878693120
RING_Z = 29252580


def device_at(turn):
    place = turn >> 3
    x = ((turn >> 1) & 3) ^ ((place & 1) * 3)
    y = (RING_Y >> (place * 2)) & 3
    z = (RING_Z >> (place * 2)) & 3
    return z * 32 + y * 8 + x * 2 + (turn & 1)


def pack_kernel(
    emb_ref, cluster_ref, rank_ref, out_ref, place_ref, raw, ids, left, right, arrived
):
    loads = [
        pltpu.make_async_copy(cluster_ref, ids.at[0], arrived.at[0]),
        pltpu.make_async_copy(rank_ref, ids.at[1], arrived.at[1]),
        pltpu.make_async_copy(emb_ref, raw, arrived.at[2]),
    ]
    for load in loads:
        load.start()

    loads[0].wait()
    cluster = ids[0]
    loads[1].wait()
    rank = ids[1]
    home = cluster & (N - 1)
    member = cluster // N

    which = iota((N, ROWS), 0)
    at_home = which == home
    at_home_b = flag(at_home)
    row, column = iota((N, N), 0), iota((N, N), 1)
    upper = flag(row < column)
    count = dot_nt(jnp.ones((8, ROWS), BF16), at_home_b)
    chunks = jnp.concatenate([at_home_b[:, c * 128 : (c + 1) * 128] for c in range(8)], axis=0)
    running = dot(chunks, jnp.concatenate([upper, jnp.ones((N, N), BF16)], axis=1))
    totals = [running[c * 128 : (c + 1) * 128, 128:] for c in range(8)]
    total = sum(totals[1:], totals[0])

    over = total - float(SLOTS)
    below = dot(flag(row > column), over.astype(BF16))
    along = dot((count - float(SLOTS)).astype(BF16), upper)
    round_trip = float(ROWS - SLOTS * N)
    ahead = below + jnp.max(
        jnp.where(column < row, 0.0, round_trip) - along[:1], axis=1, keepdims=True
    )
    ahead = jnp.maximum(ahead, 0.0)
    queue = along[:1] + count[:1] - float(SLOTS)
    queue = queue + jnp.max(
        jnp.where(row <= column, 0.0, round_trip) - below, axis=0, keepdims=True
    )
    queue = jnp.maximum(queue, 0.0)

    before = ahead
    turn = []
    for c in range(8):
        part = running[c * 128 : (c + 1) * 128, :128]
        turn.append(
            jnp.sum(
                jnp.where(at_home[:, c * 128 : (c + 1) * 128], part + before, 0.0),
                axis=0,
                keepdims=True,
            )
        )
        before = before + totals[c]
    offset = jnp.concatenate(turn, axis=1)
    hops = jnp.floor((offset + 0.5) * (1.0 / SLOTS))
    slot = (offset - hops * SLOTS).astype(I32)
    hops = hops.astype(I32)
    target = device_at((home + hops) & (N - 1))
    place_ref[0:1, :] = device_at(home)
    place_ref[1:2, :] = jnp.minimum(hops, 7) * 16 + slot

    loads[2].wait()

    def unit_rows(chosen):
        wide = dot(chosen, raw[...])
        return wide * lax.rsqrt(jnp.sum(wide * wide, axis=-1, keepdims=True) + 1e-06)

    def spread(value):
        return jnp.broadcast_to(value, (16, ROWS))

    value = jnp.concatenate(
        [
            spread(member + 1),
            spread(hops),
            spread(rank & 255),
            spread((rank >> 8) & 255),
            spread(rank >> 16),
            jnp.zeros((48, ROWS), I32),
        ],
        axis=0,
    )
    value = jnp.where((iota((META, ROWS), 0) & 15) == slot, value, 0)
    meta = dot_nt(flag(which == target), value.astype(F32).astype(BF16))
    left[pl.ds(6, N, stride=8), :] = meta
    right[pl.ds(6, N, stride=8), :] = jnp.broadcast_to(jnp.minimum(queue, 255.0), (N, 128))
    left[pl.ds(7, N, stride=8), :] = jnp.zeros((N, 128), F32)
    right[pl.ds(7, N, stride=8), :] = jnp.zeros((N, 128), F32)
    extra_row = jnp.where(slot >= 8, (slot - 8) * N + target, -1)
    late = unit_rows(flag(iota((EXTRA, ROWS), 0) == extra_row))
    for k in range(2):
        for piece in range(3):
            rows = late[k * N : (k + 1) * N, piece * 256 : (piece + 1) * 256]
            left[pl.ds(2 * piece + k, N, stride=8), :] = rows[:, :128]
            right[pl.ds(2 * piece + k, N, stride=8), :] = rows[:, 128:]
    out_ref[:, D : D + 128] = left[...].astype(BF16)
    out_ref[:, D + 128 :] = right[...].astype(BF16)

    main_row = jnp.where(slot < 8, target * 8 + slot, -1)
    for b in range(4):
        chosen = flag(iota((256, ROWS), 0) == main_row - b * 256)
        out_ref[b * 256 : (b + 1) * 256, :D] = unit_rows(chosen).astype(BF16)


def pack(emb, cluster, rank):
    return pl.pallas_call(
        pack_kernel,
        in_specs=[pl.BlockSpec(memory_space=pl.ANY)] * 3,
        out_shape=(
            jax.ShapeDtypeStruct((MAIN, D + 256), BF16),
            jax.ShapeDtypeStruct((2, ROWS), I32),
        ),
        scratch_shapes=[
            pltpu.VMEM((ROWS, D), BF16),
            pltpu.VMEM((2, 1, ROWS), I32),
            pltpu.VMEM((MAIN, 128), F32),
            pltpu.VMEM((MAIN, 128), F32),
            pltpu.SemaphoreType.DMA((3,)),
        ],
        compiler_params=LIMIT,
        name="pack",
    )(emb, cluster.reshape(1, ROWS), rank.reshape(1, ROWS))


def unpack_kernel(got_ref, late_ref, meta_ref, near_ref, far_ref, bad_ref, left, right):
    left[...] = got_ref[:, D : D + 128].astype(F32)
    right[...] = got_ref[:, D + 128 :].astype(F32)
    for k in range(2):
        for piece in range(3):
            for half, ref in enumerate((left, right)):
                at = piece * 256 + half * 128
                late_ref[k * N : (k + 1) * N, at : at + 128] = ref[
                    pl.ds(2 * piece + k, N, stride=8), :
                ].astype(BF16)
    meta = left[pl.ds(6, N, stride=8), :]
    queue = right[pl.ds(6, N, stride=8), :]
    meta_ref[...] = meta

    over_near = jnp.sum(jnp.minimum(queue, float(SLOTS)), axis=0, keepdims=True) - NEAR
    over_far = (
        jnp.sum(jnp.clip(queue - SLOTS, 0.0, float(SLOTS)), axis=0, keepdims=True) - FAR
    )
    over_long = jnp.max(queue, axis=0, keepdims=True) - 2.0 * SLOTS
    worst = jnp.maximum(jnp.maximum(over_near, over_far), over_long)
    bad_ref[...] = jnp.where(jnp.max(worst, axis=1, keepdims=True) > 0.0, 1, 0)

    lane = iota((N, N), 1)
    hops = pltpu.roll(meta, N - 16, 1)
    moves = (lane < SLOTS) & (meta > 0.0)
    one = flag(moves & (hops == 1.0))
    two = flag(moves & (hops == 2.0))
    each = dot_nt(jnp.ones((8, N), BF16), jnp.concatenate([one, two], axis=0))
    first = dot(
        jnp.concatenate([each[:, :N], each[:, N:]], axis=0).astype(BF16),
        flag(iota((N, N), 0) < iota((N, N), 1)),
    )
    count_one, count_two = each[0:1, :N], each[0:1, N:]
    first_one, first_two = first[0:1], first[8:9]

    def rows_of(length, first, count, skip):
        line = iota((length, N), 0).astype(F32)
        mine = (line >= first) & (line < first + count)
        source = jnp.sum(jnp.where(mine, iota((length, N), 1).astype(F32), 0.0), 1, keepdims=True)
        place = jnp.sum(jnp.where(mine, line - first + skip, 0.0), 1, keepdims=True)
        any_row = line[:, :1] < jnp.sum(count, 1, keepdims=True)
        return flag(mine), source.astype(I32), place.astype(I32), any_row

    near = rows_of(NEAR, first_one, count_one, count_two)
    far = rows_of(FAR, first_two, count_two, 0.0)
    mine, source, slot = (jnp.concatenate([a, b], axis=0) for a, b in zip(near[:3], far[:3]))
    used = jnp.concatenate([near[3].astype(I32), far[3].astype(I32)], axis=0) > 0

    at_main = jnp.where(used & (slot < 8), source * 8 + slot, -1)
    at_late = jnp.where(used & (slot >= 8), (slot - 8) * N + source, -1)
    sent = dot(flag(iota((MOVED, MAIN), 1) == at_main), got_ref[:, :D]) + dot(
        flag(iota((MOVED, EXTRA), 1) == at_late), late_ref[...]
    )
    sent = sent.astype(BF16)
    card = dot(mine, meta.astype(BF16))
    lanes = iota((MOVED, META), 1)
    card = jnp.where((lanes & 15) == slot, card, 0.0)
    card = jnp.where(lanes == 96, source.astype(F32), card)
    card = jnp.where(lanes == 97, slot.astype(F32), card).astype(BF16)
    near_ref[:, :D] = sent[:NEAR]
    near_ref[:, D:] = card[:NEAR]
    far_ref[:, :D] = sent[NEAR:]
    far_ref[:, D:] = card[NEAR:]


def unpack(got):
    return pl.pallas_call(
        unpack_kernel,
        out_shape=(
            jax.ShapeDtypeStruct((EXTRA, D), BF16),
            jax.ShapeDtypeStruct((N, META), F32),
            jax.ShapeDtypeStruct((NEAR, D + META), BF16),
            jax.ShapeDtypeStruct((FAR, D + META), BF16),
            jax.ShapeDtypeStruct((1, 1), I32),
        ),
        scratch_shapes=[pltpu.VMEM((MAIN, 128), F32), pltpu.VMEM((MAIN, 128), F32)],
        compiler_params=LIMIT,
        name="unpack",
    )(got)


RANK = ((2, 1.0), (3, 256.0), (4, 65536.0))
CLUSTER = ((0, 1.0), (1, -16.0))


def local_kernel(got_ref, late_ref, meta_ref, row_ref, best_ref, own, column):
    meta = meta_ref[...]
    spread = dot(flag((iota((MAIN, N), 0) >> 3) == iota((MAIN, N), 1)), meta.astype(BF16))
    own[:MAIN, :] = jnp.where(
        (iota((MAIN, N), 1) & 15) == (iota((MAIN, N), 0) & 7), spread, 0.0
    ).astype(BF16)
    lane = iota((N, N), 1) & 15
    for k in range(2):
        own[MAIN + k * N : MAIN + (k + 1) * N, :] = jnp.where(lane == 8 + k, meta, 0.0).astype(BF16)
    row_ref[...] = dot_nt(
        jnp.concatenate([weights(RANK, (8, N), 1), weights(CLUSTER, (8, N), 1)], axis=0), own[...]
    )
    column[...] = dot(
        own[...],
        jnp.concatenate([weights(RANK, (N, N), 0), weights(CLUSTER, (N, N), 0)], axis=1),
    )
    best_ref[...] = jnp.full((8, ALL), -1.0, F32)

    def rows_of(b):
        if b * 256 < MAIN:
            return got_ref[b * 256 : (b + 1) * 256, :D]
        return late_ref[...]

    blocks = ALL // 256
    for i in range(blocks):
        rank = column[i * 256 : (i + 1) * 256, :128]
        cluster = column[i * 256 : (i + 1) * 256, 128:]
        rank = jnp.concatenate([rank, rank], axis=1)
        cluster = jnp.concatenate([cluster, cluster], axis=1)
        for j in range(blocks):
            across = slice(j * 256, (j + 1) * 256)
            similar = dot_nt(rows_of(i), rows_of(j))
            earlier = (cluster == row_ref[8:9, across]) & (rank < row_ref[0:1, across])
            kept = jnp.where(earlier, similar, -1.0)
            best_ref[:, across] = jnp.maximum(
                best_ref[:, across], jnp.max(kept.reshape(32, 8, 256), axis=0)
            )


def local_best(got, late, meta):
    return pl.pallas_call(
        local_kernel,
        out_shape=(
            jax.ShapeDtypeStruct((16, ALL), F32),
            jax.ShapeDtypeStruct((8, ALL), F32),
        ),
        scratch_shapes=[pltpu.VMEM((ALL, N), BF16), pltpu.VMEM((ALL, 256), F32)],
        compiler_params=LIMIT,
        cost_estimate=pl.CostEstimate(
            flops=2 * ALL * ALL * D, bytes_accessed=4 * ALL * D, transcendentals=0
        ),
        name="local_best",
    )(got, late, meta)


def cross_kernel(got_ref, late_ref, row_ref, best_ref, near_ref, far_ref, out_ref, moved):
    moved[0:NEAR, :] = near_ref[...]
    moved[NEAR:, :] = far_ref[...]
    card = moved[:, D:]
    column = dot(
        card,
        jnp.concatenate(
            [
                weights(RANK, (META, 128), 0),
                weights(CLUSTER[:1], (META, 128), 0),
                weights(((96, 1.0),), (META, 128), 0, 1),
                weights(((97, 1.0),), (META, 128), 0, 1),
            ],
            axis=1,
        ),
    )
    rank, cluster = column[:, :128], column[:, 128:256]
    source, slot = column[:, 256:384].astype(I32), column[:, 384:].astype(I32)
    moved_row = dot_nt(
        jnp.concatenate([weights(RANK, (8, META), 1), weights(CLUSTER[:1], (8, META), 1)], axis=0),
        card,
    )
    rank2 = jnp.concatenate([rank, rank], axis=1)
    cluster2 = jnp.concatenate([cluster, cluster], axis=1)

    unit = moved[:, :D]
    arrived = jnp.full((MOVED, 256), -1.0, F32)
    bests = []
    for j in range(ALL // 256):
        across = slice(j * 256, (j + 1) * 256)
        rows = got_ref[across, :D] if j * 256 < MAIN else late_ref[...]
        similar = dot_nt(unit, rows)
        same = cluster2 == row_ref[8:9, across]
        earlier = rank2 < row_ref[0:1, across]
        kept = jnp.where(same & earlier, similar, -1.0)
        here = jnp.maximum(best_ref[:, across], jnp.max(kept.reshape(MOVED // 8, 8, 256), axis=0))
        bests.append(jnp.max(here, axis=0, keepdims=True))
        later = rank2 > row_ref[0:1, across]
        arrived = jnp.maximum(arrived, jnp.where(same & later, similar, -1.0))
    similar = dot_nt(unit, unit)
    later = (cluster2[:, :MOVED] == moved_row[8:9]) & (rank2[:, :MOVED] > moved_row[0:1])
    arrived = jnp.maximum(
        jnp.max(arrived, axis=1, keepdims=True),
        jnp.max(jnp.where(later, similar, -1.0), axis=1, keepdims=True),
    )

    main = jnp.concatenate(bests[: MAIN // 256], axis=1)
    main = jnp.where((iota((8, MAIN), 1) & 7) == iota((8, MAIN), 0), main, 0.0)
    of_sender = flag((iota((MAIN, N), 0) >> 3) == iota((MAIN, N), 1))
    answers = sum(dot(part, of_sender) for part in parts(main))
    late = bests[MAIN // 256]
    answers = jnp.concatenate(
        [answers, late[:, :N], late[:, N:], jnp.zeros((N - SLOTS, N), F32)], axis=0
    )
    hop = jnp.where(iota((MOVED, N), 0) < NEAR, 16, 32)
    by_lane = jnp.where((cluster > 0.0) & (iota((MOVED, N), 1) == hop + slot), arrived, 0.0)
    sender = flag((cluster > 0.0) & (iota((MOVED, N), 1) == source), F32).T.astype(BF16)
    out_ref[...] = answers.T + sum(dot(sender, part) for part in parts(by_lane))


def cross_best(got, late, row, best, near, far):
    return pl.pallas_call(
        cross_kernel,
        out_shape=jax.ShapeDtypeStruct((N, N), F32),
        scratch_shapes=[pltpu.VMEM((MOVED, D + META), BF16)],
        compiler_params=LIMIT,
        name="cross_best",
    )(got, late, row, best, near, far)


def pick_kernel(back_ref, place_ref, out_ref):
    home = place_ref[0:1, :]
    lane = place_ref[1:2, :]
    at_home = flag(iota((N, ROWS), 0) == home)
    table = sum(dot(part, at_home) for part in parts(back_ref[...].T[:48]))
    out_ref[...] = jnp.sum(
        jnp.where(iota((48, ROWS), 0) == lane, table, 0.0), axis=0, keepdims=True
    )


def pick(back, place):
    return pl.pallas_call(
        pick_kernel,
        out_shape=jax.ShapeDtypeStruct((1, ROWS), F32),
        compiler_params=LIMIT,
        name="pick",
    )(back, place)


def passed_along(array, by):
    return lax.ppermute(array, "dev", [(i, (i + by) % N) for i in range(N)])


def moved_back(array, by):
    pairs = [(device_at(i), device_at((i - by) % N)) for i in range(N)]
    return lax.ppermute(array, "dev", pairs)


def swapped(array):
    return lax.all_to_all(array, "dev", split_axis=0, concat_axis=0, tiled=True)


def paired_best(left, right):
    left_unit, left_cluster, left_rank = left
    right_unit, right_cluster, right_rank = right
    block_rows = 512
    block_count = left_unit.shape[0] // block_rows
    blocked = (
        left_unit.reshape(block_count, block_rows, D),
        left_cluster.reshape(block_count, block_rows),
        left_rank.reshape(block_count, block_rows),
    )

    def advance(carry, pieces):
        unit, cluster, rank = pieces
        similar = dot_nt(unit, right_unit)
        same = (cluster[:, None] == right_cluster[None, :]) & (right_cluster[None, :] >= 0)
        earlier = same & (right_rank[None, :] < rank[:, None])
        return carry, jnp.max(jnp.where(earlier, similar, -1.0), axis=1)

    return lax.scan(advance, 0, blocked)[1].reshape(-1)


def by_pools(emb, cluster, rank):
    capacity = 2 * ROWS // N
    pool_rows = N * capacity
    wide = emb.astype(F32)
    unit = (wide * lax.rsqrt(jnp.sum(wide * wide, axis=-1, keepdims=True) + 1e-06)).astype(BF16)
    target = (cluster % N + rank % 2) % N
    one_hot = (target[:, None] == jnp.arange(N, dtype=I32)[None, :]).astype(I32)
    slot = jnp.sum(jnp.cumsum(one_hot, axis=0) * one_hot, axis=1) - 1
    placing = target * capacity + slot
    received = (
        swapped(jnp.zeros((pool_rows, D), BF16).at[placing].set(unit)),
        swapped(jnp.full((pool_rows,), -1, I32).at[placing].set(cluster)),
        swapped(jnp.zeros((pool_rows,), I32).at[placing].set(rank)),
    )
    best = paired_best(received, received)
    for by in (1, -1):
        other = tuple(passed_along(part, by) for part in received)
        best = jnp.maximum(best, paired_best(received, other))
    return swapped(best)[placing]


def per_device(emb, cluster, rank):
    packed, place = pack(emb, cluster, rank)
    got = swapped(packed.reshape(N, 8, D + 256)).reshape(MAIN, D + 256)
    late, meta, near, far, bad = unpack(got)
    near = moved_back(near, 1)
    far = moved_back(far, 2)
    row, best = local_best(got, late, meta)
    row, bad = lax.optimization_barrier((row, bad))
    slow = bad[0, 0] > 0
    row, slow = lax.optimization_barrier((row, slow))
    answers = cross_best(got, late, row, best, near, far)
    back = swapped(answers.reshape(N, 1, N)).reshape(N, N)
    back, slow, emb, cluster, rank = lax.optimization_barrier((back, slow, emb, cluster, rank))
    nearest = pick(back, place).reshape(ROWS)
    return lax.cond(
        slow,
        by_pools,
        lambda emb, cluster, rank: nearest,
        emb,
        cluster,
        rank,
    )


def solution(mesh):
    placed = (P("dev", None), P("dev"), P("dev"))
    return jax.shard_map(
        per_device, mesh=mesh, in_specs=placed, out_specs=P("dev"), check_vma=False
    )
```

```python
import jax
import jax.numpy as jnp
from jax import lax
from jax.experimental import pallas as pl
from jax.experimental.pallas import tpu as pltpu
from jax.sharding import PartitionSpec as P

F32 = jnp.float32
BF16 = jnp.bfloat16
I32 = jnp.int32

N = 128
ROWS = 1024
D = 768
SLOTS = 10
MAIN = 8 * N
EXTRA = 2 * N
ALL = MAIN + EXTRA
NEAR = 144
FAR = 16
MOVED = NEAR + FAR
META = 128
LIMIT = pltpu.CompilerParams(vmem_limit_bytes=20 * 1024 * 1024)


def iota(shape, dim):
    return lax.broadcasted_iota(I32, shape, dim)


def flag(mask, dtype=BF16):
    return jnp.where(mask, 1.0, 0.0).astype(dtype)


def dot(a, b):
    return jnp.dot(a, b, preferred_element_type=F32)


def dot_nt(a, b):
    return lax.dot_general(a, b, (((1,), (1,)), ((), ())), preferred_element_type=F32)


def parts(a):
    high = a.astype(BF16)
    rest = a - high.astype(F32)
    middle = rest.astype(BF16)
    return high, middle, (rest - middle.astype(F32)).astype(BF16)


def weights(rows, shape, dim, size=16):
    group = iota(shape, dim) // size
    weight = jnp.zeros(shape, F32)
    for at, by in rows:
        weight = jnp.where(group == at, by, weight)
    return weight.astype(BF16)


RING_Y = 1878693120
RING_Z = 29252580


def device_at(turn):
    place = turn >> 3
    x = ((turn >> 1) & 3) ^ ((place & 1) * 3)
    y = (RING_Y >> (place * 2)) & 3
    z = (RING_Z >> (place * 2)) & 3
    return z * 32 + y * 8 + x * 2 + (turn & 1)


def pack_kernel(
    emb_ref, cluster_ref, rank_ref, out_ref, place_ref, raw, ids, left, right, arrived
):
    loads = [
        pltpu.make_async_copy(cluster_ref, ids.at[0], arrived.at[0]),
        pltpu.make_async_copy(rank_ref, ids.at[1], arrived.at[1]),
        pltpu.make_async_copy(emb_ref, raw, arrived.at[2]),
    ]
    for load in loads:
        load.start()

    loads[0].wait()
    cluster = ids[0]
    loads[1].wait()
    rank = ids[1]
    home = cluster & (N - 1)
    member = cluster // N

    which = iota((N, ROWS), 0)
    at_home = which == home
    at_home_b = flag(at_home)
    row, column = iota((N, N), 0), iota((N, N), 1)
    upper = flag(row < column)
    count = dot_nt(jnp.ones((8, ROWS), BF16), at_home_b)
    chunks = jnp.concatenate([at_home_b[:, c * 128 : (c + 1) * 128] for c in range(8)], axis=0)
    running = dot(chunks, jnp.concatenate([upper, jnp.ones((N, N), BF16)], axis=1))
    totals = [running[c * 128 : (c + 1) * 128, 128:] for c in range(8)]
    total = sum(totals[1:], totals[0])

    over = total - float(SLOTS)
    below = dot(flag(row > column), over.astype(BF16))
    along = dot((count - float(SLOTS)).astype(BF16), upper)
    round_trip = float(ROWS - SLOTS * N)
    ahead = below + jnp.max(
        jnp.where(column < row, 0.0, round_trip) - along[:1], axis=1, keepdims=True
    )
    ahead = jnp.maximum(ahead, 0.0)
    queue = along[:1] + count[:1] - float(SLOTS)
    queue = queue + jnp.max(
        jnp.where(row <= column, 0.0, round_trip) - below, axis=0, keepdims=True
    )
    queue = jnp.maximum(queue, 0.0)

    before = ahead
    turn = []
    for c in range(8):
        part = running[c * 128 : (c + 1) * 128, :128]
        turn.append(
            jnp.sum(
                jnp.where(at_home[:, c * 128 : (c + 1) * 128], part + before, 0.0),
                axis=0,
                keepdims=True,
            )
        )
        before = before + totals[c]
    offset = jnp.concatenate(turn, axis=1)
    hops = jnp.floor((offset + 0.5) * (1.0 / SLOTS))
    slot = (offset - hops * SLOTS).astype(I32)
    hops = hops.astype(I32)
    target = device_at((home + hops) & (N - 1))
    place_ref[0:1, :] = device_at(home)
    place_ref[1:2, :] = jnp.minimum(hops, 7) * 16 + slot

    loads[2].wait()

    def unit_rows(chosen):
        wide = dot(chosen, raw[...])
        return wide * lax.rsqrt(jnp.sum(wide * wide, axis=-1, keepdims=True) + 1e-06)

    def spread(value):
        return jnp.broadcast_to(value, (16, ROWS))

    value = jnp.concatenate(
        [
            spread(member + 1),
            spread(hops),
            spread(rank & 255),
            spread((rank >> 8) & 255),
            spread(rank >> 16),
            jnp.zeros((48, ROWS), I32),
        ],
        axis=0,
    )
    value = jnp.where((iota((META, ROWS), 0) & 15) == slot, value, 0)
    meta = dot_nt(flag(which == target), value.astype(F32).astype(BF16))
    left[pl.ds(6, N, stride=8), :] = meta
    right[pl.ds(6, N, stride=8), :] = jnp.broadcast_to(jnp.minimum(queue, 255.0), (N, 128))
    left[pl.ds(7, N, stride=8), :] = jnp.zeros((N, 128), F32)
    right[pl.ds(7, N, stride=8), :] = jnp.zeros((N, 128), F32)
    extra_row = jnp.where(slot >= 8, (slot - 8) * N + target, -1)
    late = unit_rows(flag(iota((EXTRA, ROWS), 0) == extra_row))
    for k in range(2):
        for piece in range(3):
            rows = late[k * N : (k + 1) * N, piece * 256 : (piece + 1) * 256]
            left[pl.ds(2 * piece + k, N, stride=8), :] = rows[:, :128]
            right[pl.ds(2 * piece + k, N, stride=8), :] = rows[:, 128:]
    out_ref[:, D : D + 128] = left[...].astype(BF16)
    out_ref[:, D + 128 :] = right[...].astype(BF16)

    main_row = jnp.where(slot < 8, target * 8 + slot, -1)
    for b in range(4):
        chosen = flag(iota((256, ROWS), 0) == main_row - b * 256)
        out_ref[b * 256 : (b + 1) * 256, :D] = unit_rows(chosen).astype(BF16)


def pack(emb, cluster, rank):
    return pl.pallas_call(
        pack_kernel,
        in_specs=[pl.BlockSpec(memory_space=pl.ANY)] * 3,
        out_shape=(
            jax.ShapeDtypeStruct((MAIN, D + 256), BF16),
            jax.ShapeDtypeStruct((2, ROWS), I32),
        ),
        scratch_shapes=[
            pltpu.VMEM((ROWS, D), BF16),
            pltpu.VMEM((2, 1, ROWS), I32),
            pltpu.VMEM((MAIN, 128), F32),
            pltpu.VMEM((MAIN, 128), F32),
            pltpu.SemaphoreType.DMA((3,)),
        ],
        compiler_params=LIMIT,
        name="pack",
    )(emb, cluster.reshape(1, ROWS), rank.reshape(1, ROWS))


def unpack_kernel(got_ref, late_ref, meta_ref, near_ref, far_ref, bad_ref, left, right):
    left[...] = got_ref[:, D : D + 128].astype(F32)
    right[...] = got_ref[:, D + 128 :].astype(F32)
    for k in range(2):
        for piece in range(3):
            for half, ref in enumerate((left, right)):
                at = piece * 256 + half * 128
                late_ref[k * N : (k + 1) * N, at : at + 128] = ref[
                    pl.ds(2 * piece + k, N, stride=8), :
                ].astype(BF16)
    meta = left[pl.ds(6, N, stride=8), :]
    queue = right[pl.ds(6, N, stride=8), :]
    meta_ref[...] = meta

    over_near = jnp.sum(jnp.minimum(queue, float(SLOTS)), axis=0, keepdims=True) - NEAR
    over_far = (
        jnp.sum(jnp.clip(queue - SLOTS, 0.0, float(SLOTS)), axis=0, keepdims=True) - FAR
    )
    over_long = jnp.max(queue, axis=0, keepdims=True) - 2.0 * SLOTS
    bad_ref[0, 0] = (
        jnp.max(jnp.maximum(jnp.maximum(over_near, over_far), over_long)) > 0.0
    ).astype(I32)

    lane = iota((N, N), 1)
    hops = pltpu.roll(meta, N - 16, 1)
    moves = (lane < SLOTS) & (meta > 0.0)
    one = flag(moves & (hops == 1.0))
    two = flag(moves & (hops == 2.0))
    each = dot_nt(jnp.ones((8, N), BF16), jnp.concatenate([one, two], axis=0))
    first = dot(
        jnp.concatenate([each[:, :N], each[:, N:]], axis=0).astype(BF16),
        flag(iota((N, N), 0) < iota((N, N), 1)),
    )
    count_one, count_two = each[0:1, :N], each[0:1, N:]
    first_one, first_two = first[0:1], first[8:9]

    def rows_of(length, first, count, skip):
        line = iota((length, N), 0).astype(F32)
        mine = (line >= first) & (line < first + count)
        source = jnp.sum(jnp.where(mine, iota((length, N), 1).astype(F32), 0.0), 1, keepdims=True)
        place = jnp.sum(jnp.where(mine, line - first + skip, 0.0), 1, keepdims=True)
        any_row = line[:, :1] < jnp.sum(count, 1, keepdims=True)
        return flag(mine), source.astype(I32), place.astype(I32), any_row

    near = rows_of(NEAR, first_one, count_one, count_two)
    far = rows_of(FAR, first_two, count_two, 0.0)
    mine, source, slot = (jnp.concatenate([a, b], axis=0) for a, b in zip(near[:3], far[:3]))
    used = jnp.concatenate([near[3].astype(I32), far[3].astype(I32)], axis=0) > 0

    at_main = jnp.where(used & (slot < 8), source * 8 + slot, -1)
    at_late = jnp.where(used & (slot >= 8), (slot - 8) * N + source, -1)
    sent = dot(flag(iota((MOVED, MAIN), 1) == at_main), got_ref[:, :D]) + dot(
        flag(iota((MOVED, EXTRA), 1) == at_late), late_ref[...]
    )
    sent = sent.astype(BF16)
    card = dot(mine, meta.astype(BF16))
    lanes = iota((MOVED, META), 1)
    card = jnp.where((lanes & 15) == slot, card, 0.0)
    card = jnp.where(lanes == 96, source.astype(F32), card)
    card = jnp.where(lanes == 97, slot.astype(F32), card).astype(BF16)
    near_ref[:, :D] = sent[:NEAR]
    near_ref[:, D:] = card[:NEAR]
    far_ref[:, :D] = sent[NEAR:]
    far_ref[:, D:] = card[NEAR:]


def unpack(got):
    return pl.pallas_call(
        unpack_kernel,
        out_shape=(
            jax.ShapeDtypeStruct((EXTRA, D), BF16),
            jax.ShapeDtypeStruct((N, META), F32),
            jax.ShapeDtypeStruct((NEAR, D + META), BF16),
            jax.ShapeDtypeStruct((FAR, D + META), BF16),
            jax.ShapeDtypeStruct((1, 1), I32),
        ),
        out_specs=(pl.BlockSpec(memory_space=pltpu.VMEM),) * 4
        + (pl.BlockSpec(memory_space=pltpu.SMEM),),
        scratch_shapes=[pltpu.VMEM((MAIN, 128), F32), pltpu.VMEM((MAIN, 128), F32)],
        compiler_params=LIMIT,
        name="unpack",
    )(got)


RANK = ((2, 1.0), (3, 256.0), (4, 65536.0))
CLUSTER = ((0, 1.0), (1, -16.0))


def local_kernel(got_ref, late_ref, meta_ref, row_ref, best_ref, own, column):
    meta = meta_ref[...]
    spread = dot(flag((iota((MAIN, N), 0) >> 3) == iota((MAIN, N), 1)), meta.astype(BF16))
    own[:MAIN, :] = jnp.where(
        (iota((MAIN, N), 1) & 15) == (iota((MAIN, N), 0) & 7), spread, 0.0
    ).astype(BF16)
    lane = iota((N, N), 1) & 15
    for k in range(2):
        own[MAIN + k * N : MAIN + (k + 1) * N, :] = jnp.where(lane == 8 + k, meta, 0.0).astype(BF16)
    row_ref[...] = dot_nt(
        jnp.concatenate([weights(RANK, (8, N), 1), weights(CLUSTER, (8, N), 1)], axis=0), own[...]
    )
    column[...] = dot(
        own[...],
        jnp.concatenate([weights(RANK, (N, N), 0), weights(CLUSTER, (N, N), 0)], axis=1),
    )
    def rows_of(b):
        if b * 256 < MAIN:
            return got_ref[b * 256 : (b + 1) * 256, :D]
        return late_ref[...]

    for j in range(ALL // 256):
        across = slice(j * 256, (j + 1) * 256)
        held = rows_of(j)
        best = jnp.full((8, 256), -1.0, F32)
        for first, rows in ((0, got_ref[:, :D]), (MAIN, late_ref[...])):
            similar = dot_nt(rows, held)
            for i in range(rows.shape[0] // 256):
                at = slice(first + i * 256, first + (i + 1) * 256)
                rank = column[at, :128]
                cluster = column[at, 128:]
                rank = jnp.concatenate([rank, rank], axis=1)
                cluster = jnp.concatenate([cluster, cluster], axis=1)
                earlier = (cluster == row_ref[8:9, across]) & (rank < row_ref[0:1, across])
                kept = jnp.where(earlier, similar[i * 256 : (i + 1) * 256], -1.0)
                best = jnp.maximum(best, jnp.max(kept.reshape(32, 8, 256), axis=0))
        best_ref[:, across] = best


def local_best(got, late, meta):
    return pl.pallas_call(
        local_kernel,
        out_shape=(
            jax.ShapeDtypeStruct((16, ALL), F32),
            jax.ShapeDtypeStruct((8, ALL), F32),
        ),
        scratch_shapes=[pltpu.VMEM((ALL, N), BF16), pltpu.VMEM((ALL, 256), F32)],
        compiler_params=LIMIT,
        cost_estimate=pl.CostEstimate(
            flops=2 * ALL * ALL * D, bytes_accessed=4 * ALL * D, transcendentals=0
        ),
        name="local_best",
    )(got, late, meta)


def cross_kernel(got_ref, late_ref, row_ref, best_ref, near_ref, far_ref, out_ref, moved):
    moved[0:NEAR, :] = near_ref[...]
    moved[NEAR:, :] = far_ref[...]
    card = moved[:, D:]
    column = dot(
        card,
        jnp.concatenate(
            [
                weights(RANK, (META, 128), 0),
                weights(CLUSTER[:1], (META, 128), 0),
                weights(((96, 1.0),), (META, 128), 0, 1),
                weights(((97, 1.0),), (META, 128), 0, 1),
            ],
            axis=1,
        ),
    )
    rank, cluster = column[:, :128], column[:, 128:256]
    source, slot = column[:, 256:384].astype(I32), column[:, 384:].astype(I32)
    moved_row = dot_nt(
        jnp.concatenate([weights(RANK, (8, META), 1), weights(CLUSTER[:1], (8, META), 1)], axis=0),
        card,
    )
    rank2 = jnp.concatenate([rank, rank], axis=1)
    cluster2 = jnp.concatenate([cluster, cluster], axis=1)

    unit = moved[:, :D]
    arrived = jnp.full((MOVED, 256), -1.0, F32)
    bests = []
    for j in range(ALL // 256):
        across = slice(j * 256, (j + 1) * 256)
        rows = got_ref[across, :D] if j * 256 < MAIN else late_ref[...]
        similar = dot_nt(unit, rows)
        same = cluster2 == row_ref[8:9, across]
        earlier = rank2 < row_ref[0:1, across]
        kept = jnp.where(same & earlier, similar, -1.0)
        here = jnp.maximum(best_ref[:, across], jnp.max(kept.reshape(MOVED // 8, 8, 256), axis=0))
        bests.append(jnp.max(here, axis=0, keepdims=True))
        later = rank2 > row_ref[0:1, across]
        arrived = jnp.maximum(arrived, jnp.where(same & later, similar, -1.0))
    similar = dot_nt(unit, unit)
    later = (cluster2[:, :MOVED] == moved_row[8:9]) & (rank2[:, :MOVED] > moved_row[0:1])
    arrived = jnp.maximum(
        jnp.max(arrived, axis=1, keepdims=True),
        jnp.max(jnp.where(later, similar, -1.0), axis=1, keepdims=True),
    )

    main = jnp.concatenate(bests[: MAIN // 256], axis=1)
    main = jnp.where((iota((8, MAIN), 1) & 7) == iota((8, MAIN), 0), main, 0.0)
    of_sender = flag((iota((MAIN, N), 0) >> 3) == iota((MAIN, N), 1))
    answers = sum(dot(part, of_sender) for part in parts(main))
    late = bests[MAIN // 256]
    answers = jnp.concatenate(
        [answers, late[:, :N], late[:, N:], jnp.zeros((N - SLOTS, N), F32)], axis=0
    )
    hop = jnp.where(iota((MOVED, N), 0) < NEAR, 16, 32)
    by_lane = jnp.where((cluster > 0.0) & (iota((MOVED, N), 1) == hop + slot), arrived, 0.0)
    sender = flag((cluster > 0.0) & (iota((MOVED, N), 1) == source), F32).T.astype(BF16)
    out_ref[...] = answers.T + sum(dot(sender, part) for part in parts(by_lane))


def cross_best(got, late, row, best, near, far):
    return pl.pallas_call(
        cross_kernel,
        out_shape=jax.ShapeDtypeStruct((N, N), F32),
        scratch_shapes=[pltpu.VMEM((MOVED, D + META), BF16)],
        compiler_params=LIMIT,
        name="cross_best",
    )(got, late, row, best, near, far)


def pick_kernel(back_ref, place_ref, out_ref):
    home = place_ref[0:1, :]
    lane = place_ref[1:2, :]
    at_home = flag(iota((N, ROWS), 0) == home)
    table = sum(dot(part, at_home) for part in parts(back_ref[...].T[:48]))
    out_ref[...] = jnp.sum(
        jnp.where(iota((48, ROWS), 0) == lane, table, 0.0), axis=0, keepdims=True
    )


def pick(back, place):
    return pl.pallas_call(
        pick_kernel,
        out_shape=jax.ShapeDtypeStruct((1, ROWS), F32),
        compiler_params=LIMIT,
        name="pick",
    )(back, place)


def passed_along(array, by):
    return lax.ppermute(array, "dev", [(i, (i + by) % N) for i in range(N)])


def moved_back(array, by):
    pairs = [(device_at(i), device_at((i - by) % N)) for i in range(N)]
    return lax.ppermute(array, "dev", pairs)


def swapped(array):
    return lax.all_to_all(array, "dev", split_axis=0, concat_axis=0, tiled=True)


def paired_best(left, right):
    left_unit, left_cluster, left_rank = left
    right_unit, right_cluster, right_rank = right
    block_rows = 512
    block_count = left_unit.shape[0] // block_rows
    blocked = (
        left_unit.reshape(block_count, block_rows, D),
        left_cluster.reshape(block_count, block_rows),
        left_rank.reshape(block_count, block_rows),
    )

    def advance(carry, pieces):
        unit, cluster, rank = pieces
        similar = dot_nt(unit, right_unit)
        same = (cluster[:, None] == right_cluster[None, :]) & (right_cluster[None, :] >= 0)
        earlier = same & (right_rank[None, :] < rank[:, None])
        return carry, jnp.max(jnp.where(earlier, similar, -1.0), axis=1)

    return lax.scan(advance, 0, blocked)[1].reshape(-1)


def by_pools(emb, cluster, rank):
    capacity = 2 * ROWS // N
    pool_rows = N * capacity
    wide = emb.astype(F32)
    unit = (wide * lax.rsqrt(jnp.sum(wide * wide, axis=-1, keepdims=True) + 1e-06)).astype(BF16)
    target = (cluster % N + rank % 2) % N
    one_hot = (target[:, None] == jnp.arange(N, dtype=I32)[None, :]).astype(I32)
    slot = jnp.sum(jnp.cumsum(one_hot, axis=0) * one_hot, axis=1) - 1
    placing = target * capacity + slot
    received = (
        swapped(jnp.zeros((pool_rows, D), BF16).at[placing].set(unit)),
        swapped(jnp.full((pool_rows,), -1, I32).at[placing].set(cluster)),
        swapped(jnp.zeros((pool_rows,), I32).at[placing].set(rank)),
    )
    best = paired_best(received, received)
    for by in (1, -1):
        other = tuple(passed_along(part, by) for part in received)
        best = jnp.maximum(best, paired_best(received, other))
    return swapped(best)[placing]


def per_device(emb, cluster, rank):
    packed, place = pack(emb, cluster, rank)
    got = swapped(packed.reshape(N, 8, D + 256)).reshape(MAIN, D + 256)
    late, meta, near, far, bad = unpack(got)
    near = moved_back(near, 1)
    far = moved_back(far, 2)
    row, best = local_best(got, late, meta)
    row, bad = lax.optimization_barrier((row, bad))
    slow = bad[0, 0] > 0
    row, slow = lax.optimization_barrier((row, slow))
    answers = cross_best(got, late, row, best, near, far)
    back = swapped(answers.reshape(N, 1, N)).reshape(N, N)
    back, slow, emb, cluster, rank = lax.optimization_barrier((back, slow, emb, cluster, rank))
    nearest = pick(back, place).reshape(ROWS)
    return lax.cond(
        slow,
        by_pools,
        lambda emb, cluster, rank: nearest,
        emb,
        cluster,
        rank,
    )


def solution(mesh):
    placed = (P("dev", None), P("dev"), P("dev"))
    return jax.shard_map(
        per_device, mesh=mesh, in_specs=placed, out_specs=P("dev"), check_vma=False
    )
```
